32 devices in a mesh: slab: 2 (over y), row: 16 (over z, x, core).
Axes of the slice: x: 2, y: 2, z: 4, core: 2. Of those that a mesh axis runs over, the one named last changes fastest.
Arguments:
- rows_strip: bfloat16 [32, 2, 2, 3, 16, 512], P(('slab', 'row')), parts along dimension 0, may hold values from 0 to 1
- cols_strip: bfloat16 [32, 2, 2, 3, 16, 512], P(('slab', 'row')), parts along dimension 0, may hold values from 0 to 1
- offsets: int32 [32, 2, 4], P(('slab', 'row')), parts along dimension 0, may hold values from 0 to 15
- extents: int32 [32, 2, 4, 2], P(('slab', 'row')), parts along dimension 0, may hold values from 0 to 512, as said below
- prior: float32 [32, 2, 3, 4, 1024], P(('slab', 'row')), parts along dimension 0, may hold values from -3 to 3
Outputs:
- colour_maps: float32 [32, 2, 3, 4, 1024], P(('slab', 'row')), parts along dimension 0
- residual: float32 [32, 2, 3, 4, 1024], P(('slab', 'row')), parts along dimension 0
The draws below stay inside these ranges and needn't reach their ends.
There are 2 independent parts, one for each index of `slab`. The reference program is written for one: setup_inputs(seed, part) draws one part's arguments, and reference() takes and returns one part's arrays. A program takes and returns all parts, laid end to end along the dimension named above; each array names one. Nothing has to cross between parts.
Inputs may be any that keep to these rules, and one draw needn't show every extreme that they name: `extents`: for each tile and direction d (0 east, 1 south, 2 south-east, 3 south-west) the first entry is at most the second; for directions 2 and 3 both are at most 16.
All inputs are finite; a program needn't handle non-finite values.
Results may differ from the reference program's by a relative error of at most 0.0003.
Values may be sent and summed in bfloat16 or wider, within the bound.
A program may use at most 64 MiB of HBM per device.

```python
import jax
import jax.numpy as jnp
from jax import lax

G = 32
CELL = 16
TILE_COLS = 2
ITERS = 2
TILE_ROWS = 16
NODES = 1024
PIXELS = 512


def draw_extents(key, part):
    key = jax.random.fold_in(key, 7)
    first_key, second_key = jax.random.split(key)
    length = jnp.array([G * CELL, G * CELL, CELL, CELL], jnp.int32)
    shape = (TILE_ROWS, TILE_COLS, 4)
    start = jax.random.randint(first_key, shape, 0, length // 4 + 1)
    finish = length - jax.random.randint(second_key, shape, 0, length // 4 + 1)
    return jnp.stack([start, finish], axis=-1).astype(jnp.int32)


def with_ends(values, own_key, low, top_value):
    shape = values.shape
    spot = [jax.random.randint(jax.random.fold_in(own_key, axis), (), 0, shape[axis]) for axis in range(len(shape))]
    values = values.at[tuple(spot)].set(low)
    longest = shape.index(max(shape))
    spot[longest] = (spot[longest] + 1) % shape[longest]
    return values.at[tuple(spot)].set(top_value)


def levels(rng, dims, cuts, smallest, largest):
    level = 1.0
    for dim, parts in cuts:
        steps = jax.random.uniform(jax.random.fold_in(jax.random.fold_in(rng, 6), dim), (parts,), jnp.float32, smallest / len(cuts), largest / len(cuts))
        level = level * jnp.repeat(jnp.exp(steps), dims[dim] // parts).reshape((-1,) + (1,) * (len(dims) - 1 - dim))
    return level


def normal_values(stream_key, shape, deviation, bound, shards=(), kind=jnp.bfloat16):
    values = deviation * jax.random.normal(stream_key, shape, jnp.float32)
    if shards:
        values = values * levels(stream_key, shape, shards, -0.22, 0.18)
    return jnp.clip(values, -bound, bound).astype(kind)


def setup_inputs(seed: int = 0, part: int = 0) -> dict:
    seeds = jax.random.split(jax.random.key(seed), 6)
    part_keys = jax.random.split(jax.random.fold_in(seeds[5], part), 6)
    rows_strip = jnp.clip(1.0 * jax.random.uniform(part_keys[0], (TILE_ROWS, TILE_COLS, 2, 3, CELL, PIXELS), jnp.float32) ** levels(part_keys[0], (TILE_ROWS, TILE_COLS, 2, 3, CELL, PIXELS), ((0, 16),), -0.2, 0.2), 0.0, 1.0).astype(jnp.bfloat16)
    cols_strip = jnp.clip(1.0 * jax.random.uniform(part_keys[1], (TILE_ROWS, TILE_COLS, 2, 3, CELL, PIXELS), jnp.float32) ** levels(part_keys[1], (TILE_ROWS, TILE_COLS, 2, 3, CELL, PIXELS), ((0, 16),), -0.2, 0.2), 0.0, 1.0).astype(jnp.bfloat16)
    offsets = with_ends(jax.random.randint(part_keys[2], (TILE_ROWS, TILE_COLS, 4), 0, CELL), jax.random.fold_in(part_keys[2], 1), 0, CELL - 1).astype(jnp.int32)
    extents = draw_extents(jax.random.fold_in(jax.random.fold_in(seeds[5], part), 71), part)
    prior = normal_values(part_keys[4], (TILE_ROWS, TILE_COLS, 3, 4, NODES), 0.3, 3.0, ((0, 16),), jnp.float32)
    return dict(rows_strip=rows_strip, cols_strip=cols_strip, offsets=offsets, extents=extents, prior=prior)


PRIOR_WEIGHT = 0.5
SMOOTHNESS = 1.0
HIGH = lax.Precision.HIGHEST


def next_along(values, axis):
    tail = lax.slice_in_dim(values, 1, values.shape[axis], axis=axis)
    zero_part = jnp.zeros_like(lax.slice_in_dim(values, 0, 1, axis=axis))
    return jnp.concatenate([tail, zero_part], axis=axis)


def prev_along(values, axis):
    head = lax.slice_in_dim(values, 0, values.shape[axis] - 1, axis=axis)
    zero_part = jnp.zeros_like(lax.slice_in_dim(values, 0, 1, axis=axis))
    return jnp.concatenate([zero_part, head], axis=axis)


def augment(strip):
    values = strip.astype(jnp.float32)
    return jnp.concatenate([values, jnp.ones_like(values[..., :1, :, :])], axis=-3)


def align_strip(strip, offset):
    length = strip.shape[-1]
    positions = jnp.arange(length, dtype=jnp.int32)
    index_map = jnp.minimum(positions + offset[..., None], length - 1).astype(jnp.int32)
    index_map = jnp.broadcast_to(index_map[..., None, None, :], strip.shape)
    return jnp.take_along_axis(strip, index_map, axis=-1)


def pair_weights(offset, extent, length, exists):
    positions = jnp.arange(length, dtype=jnp.int32)
    moved = positions + offset[..., None]
    valid = (positions >= extent[..., 0:1]) & (positions < extent[..., 1:2]) & (moved < length)
    split = moved // CELL - positions // CELL
    first = jnp.where(valid & (split == 0), 1.0, 0.0).astype(jnp.float32)
    second = jnp.where(valid & (split == 1), 1.0, 0.0).astype(jnp.float32)
    return jnp.stack([first, second], axis=-2) * exists[..., None, None]


def pair_moments(strip_a, strip_b, weight):
    leading = strip_a.shape[:-3]
    cells = strip_a.shape[-1] // CELL
    shape = leading + (4, CELL, cells, CELL)
    grid_a = strip_a.reshape(shape)
    grid_b = strip_b.reshape(shape)
    mask = weight.reshape(leading + (2, 1, 1, cells, CELL))
    masked_a = grid_a[..., None, :, :, :, :] * mask
    masked_b = grid_b[..., None, :, :, :, :] * mask
    scale = 1.0 / (CELL * CELL)
    self_a = jnp.einsum('...kpwnc,...qwnc->...knpq', masked_a, grid_a, precision=HIGH) * scale
    cross = jnp.einsum('...kpwnc,...qwnc->...knpq', masked_a, grid_b, precision=HIGH) * scale
    self_b = jnp.einsum('...kpwnc,...qwnc->...knpq', masked_b, grid_b, precision=HIGH) * scale
    return (self_a, cross, self_b)


def row_moments(bottom, below_top, left_cols, right_cols, offsets, extents, has_below):
    tiles = bottom.shape[0]
    full = bottom.shape[-1]
    depth = bottom.shape[-2]
    column = jnp.arange(tiles, dtype=jnp.int32)
    has_right = jnp.where(column < tiles - 1, 1.0, 0.0).astype(jnp.float32)
    has_left = jnp.where(column > 0, 1.0, 0.0).astype(jnp.float32)
    below_flag = has_below * jnp.ones((tiles,), jnp.float32)
    east = pair_moments(augment(right_cols), align_strip(augment(next_along(left_cols, 0)), offsets[:, 0]),
                        pair_weights(offsets[:, 0], extents[:, 0], full, has_right))
    south = pair_moments(augment(bottom), align_strip(augment(below_top), offsets[:, 1]),
                         pair_weights(offsets[:, 1], extents[:, 1], full, below_flag))
    south_east = pair_moments(augment(bottom[..., full - depth:]),
                              align_strip(augment(next_along(below_top, 0)[..., :depth]), offsets[:, 2]),
                              pair_weights(offsets[:, 2], extents[:, 2], depth, below_flag * has_right))
    south_west = pair_moments(augment(bottom[..., :depth]),
                              align_strip(augment(prev_along(below_top, 0)[..., full - depth:]), offsets[:, 3]),
                              pair_weights(offsets[:, 3], extents[:, 3], depth, below_flag * has_left))
    corners = tuple(part[:, 0, 0] for part in south_east + south_west)
    return east + south + corners


def node_apply(matrix, field):
    return jnp.einsum('...pq,...cq->...cp', matrix, field, precision=HIGH)


def node_apply_t(matrix, field):
    return jnp.einsum('...pq,...cp->...cq', matrix, field, precision=HIGH)


def edge_apply(matrix, field):
    return jnp.einsum('...npq,...cqn->...cpn', matrix, field, precision=HIGH)


def edge_apply_t(matrix, field):
    return jnp.einsum('...npq,...cpn->...cqn', matrix, field, precision=HIGH)


def shift_cells(field):
    return jnp.concatenate([field[..., 1:], jnp.zeros_like(field[..., :1])], axis=-1)


def unshift_cells(field):
    return jnp.concatenate([jnp.zeros_like(field[..., :1]), field[..., :-1]], axis=-1)


def side_to_a(self_a, cross, near_a, near_b):
    result = edge_apply(self_a[..., 0, :, :, :] + self_a[..., 1, :, :, :], near_a)
    result = result - edge_apply(cross[..., 0, :, :, :], near_b)
    return result - edge_apply(cross[..., 1, :, :, :], shift_cells(near_b))


def side_to_b(cross, self_b, near_a, near_b):
    first = edge_apply(self_b[..., 0, :, :, :], near_b) - edge_apply_t(cross[..., 0, :, :, :], near_a)
    second = edge_apply(self_b[..., 1, :, :, :], shift_cells(near_b)) - edge_apply_t(cross[..., 1, :, :, :], near_a)
    return first + unshift_cells(second)


def corner_to_a(self_a, cross, near_a, near_b):
    return node_apply(self_a, near_a) - node_apply(cross, near_b)


def corner_to_b(cross, self_b, near_a, near_b):
    return node_apply(self_b, near_b) - node_apply_t(cross, near_a)


def smooth_term(field):
    down = field[..., 1:, :] - field[..., :-1, :]
    across = field[..., :, 1:] - field[..., :, :-1]
    zero_row = jnp.zeros_like(field[..., :1, :])
    zero_col = jnp.zeros_like(field[..., :, :1])
    result = jnp.concatenate([-down, zero_row], axis=-2) + jnp.concatenate([zero_row, down], axis=-2)
    return result + jnp.concatenate([-across, zero_col], axis=-1) + jnp.concatenate([zero_col, across], axis=-1)


def operate(field, moments):
    east = moments[0:3]
    south = moments[3:6]
    corner_se = moments[6:9]
    corner_sw = moments[9:12]
    result = PRIOR_WEIGHT * field + SMOOTHNESS * smooth_term(field)
    right = next_along(field, 1)
    near_a = field[..., :, -1]
    near_b = right[..., :, 0]
    result = result.at[..., :, -1].add(side_to_a(east[0], east[1], near_a, near_b))
    result = result.at[..., :, 0].add(prev_along(side_to_b(east[1], east[2], near_a, near_b), 1))
    lower = next_along(field, 0)
    near_a = field[..., -1, :]
    near_b = lower[..., 0, :]
    result = result.at[..., -1, :].add(side_to_a(south[0], south[1], near_a, near_b))
    result = result.at[..., 0, :].add(prev_along(side_to_b(south[1], south[2], near_a, near_b), 0))
    near_a = field[..., -1, -1]
    near_b = next_along(lower, 1)[..., 0, 0]
    result = result.at[..., -1, -1].add(corner_to_a(corner_se[0], corner_se[1], near_a, near_b))
    result = result.at[..., 0, 0].add(prev_along(prev_along(corner_to_b(corner_se[1], corner_se[2], near_a, near_b), 1), 0))
    near_a = field[..., -1, 0]
    near_b = prev_along(lower, 1)[..., 0, -1]
    result = result.at[..., -1, 0].add(corner_to_a(corner_sw[0], corner_sw[1], near_a, near_b))
    result = result.at[..., 0, -1].add(prev_along(next_along(corner_to_b(corner_sw[1], corner_sw[2], near_a, near_b), 1), 0))
    return result


def colour_sum(first, second):
    return jnp.sum(first * second, axis=(0, 1, 3, 4, 5))


def per_colour(values):
    return values[:, None, None, None]


def reference(rows_strip, cols_strip, offsets, extents, prior):
    tile_rows = rows_strip.shape[0]
    tile_cols = rows_strip.shape[1]
    has_below = jnp.where(jnp.arange(tile_rows) < tile_rows - 1, 1.0, 0.0).astype(jnp.float32)
    below_top = next_along(rows_strip[:, :, 0], 0)

    def per_row(items):
        return row_moments(*items)

    moments = lax.map(per_row, (rows_strip[:, :, 1], below_top, cols_strip[:, :, 0], cols_strip[:, :, 1],
                                offsets, extents, has_below))
    identity = (jnp.arange(3)[:, None] == jnp.arange(4)[None, :]).astype(jnp.float32)
    prior_grid = prior.reshape(tile_rows, tile_cols, 3, 4, G, G)
    rhs = PRIOR_WEIGHT * (identity[:, :, None, None] + prior_grid)
    solution = jnp.zeros_like(rhs)
    residual = rhs
    direction = rhs
    norm_now = colour_sum(residual, residual)
    for iteration in range(ITERS):
        image = operate(direction, moments)
        alpha = norm_now / colour_sum(direction, image)
        solution = solution + per_colour(alpha) * direction
        residual = residual - per_colour(alpha) * image
        norm_next = colour_sum(residual, residual)
        direction = residual + per_colour(norm_next / norm_now) * direction
        norm_now = norm_next
    shape = (tile_rows, tile_cols, 3, 4, G * G)
    return solution.reshape(shape), residual.reshape(shape)
```

```python
import functools

import jax
import jax.numpy as jnp
from jax import lax
from jax.experimental import pallas as pl
from jax.experimental.pallas import tpu as pltpu
from jax.sharding import PartitionSpec as P

G = 32
CELL = 16
NODES = G * G
SIDE = G * CELL
LANES = 128
KINDS = 22
ROWS = KINDS * 8
META = 32

F32 = jnp.float32
BF16 = jnp.bfloat16


def iota(shape, axis):
    return lax.broadcasted_iota(jnp.int32, shape, axis)


def roll(values, shift, axis):
    return pltpu.roll(values, shift % values.shape[axis], axis)


def dot_nt(first, second):
    return lax.dot_general(first, second, (((1,), (1,)), ((), ())), preferred_element_type=F32)


def dot_nn(first, second):
    return lax.dot_general(first, second, (((1,), (0,)), ((), ())), preferred_element_type=F32)


def thirds(values):
    high = values.astype(BF16)
    rest = values - high.astype(F32)
    middle = rest.astype(BF16)
    low = (rest - middle.astype(F32)).astype(BF16)
    return jnp.concatenate([high, middle, low], axis=0)


def joined(parts):
    size = parts.shape[0] // 3
    return parts[:size] + (parts[size : 2 * size] + parts[2 * size :])


def edge_matrix():
    lane = iota((LANES, NODES), 0)
    node = iota((LANES, NODES), 1)
    spot = lane & (G - 1)
    target = jnp.where(
        lane < G,
        NODES - G + spot,
        jnp.where(lane < 2 * G, spot, jnp.where(lane < 3 * G, spot * G + G - 1, spot * G)),
    )
    return jnp.where(node == target, 1.0, 0.0).astype(BF16)


def smooth(field):
    node = iota((1, NODES), 1)
    column = node & (G - 1)
    up = jnp.where(node >= G, 1.0, 0.0)
    down = jnp.where(node < NODES - G, 1.0, 0.0)
    left = jnp.where(column > 0, 1.0, 0.0)
    right = jnp.where(column < G - 1, 1.0, 0.0)
    total = (0.5 + up + down + left + right) * field
    total = total - up * roll(field, G, 1) - down * roll(field, -G, 1)
    return total - left * roll(field, 1, 1) - right * roll(field, -1, 1)


def meta_row(buffer, tile, direction, which, width):
    spot = META + tile * 12 + direction * 3 + which
    row = buffer[spot : spot + 1, :].astype(jnp.int32)
    return jnp.concatenate([row] * (width // LANES), axis=1)


def aligned(strip, offset):
    amount = jnp.broadcast_to(offset, strip.shape)
    for bit in range(4):
        strip = jnp.where((amount & (1 << bit)) != 0, roll(strip, -(1 << bit), 1), strip)
    return strip


def flat(strip):
    return strip.astype(F32).reshape(3 * CELL, strip.shape[-1])


def put_products(lhs, tile, start, x, y):
    width = x.shape[-1]
    x = x.reshape(3, CELL, width)
    y = y.reshape(3, CELL, width)
    products = jnp.concatenate(
        [
            x[0:1] * x,
            x[1:2] * x[1:],
            x[2:3] * x[2:],
            x,
            x[0:1] * y,
            x[1:2] * y,
            x[2:3] * y,
            y,
            jnp.ones((1, CELL, width), F32),
        ],
        axis=0,
    )
    sums = (products[:, :8] + products[:, 8:]).reshape(ROWS, width)
    high = sums.astype(BF16)
    lhs[tile, :ROWS, start : start + width] = high
    lhs[tile, ROWS:, start : start + width] = (sums - high.astype(F32)).astype(BF16)


def put_weights(weights, tile, start, base, at_b, offset, low, high, exists):
    place = iota((1, SIDE), 1)
    moved = place + offset
    valid = (place >= low) & (place < high) & (moved < SIDE)
    split = (moved >> 4) - (place >> 4)
    cell = (moved >> 4) if at_b else (place >> 4)
    target = jnp.where(valid, base + cell + LANES * split, -1)
    target = jnp.where(exists > 0, target, -1)
    hit = iota((2 * LANES, SIDE), 0) == jnp.broadcast_to(target, (2 * LANES, SIDE))
    weights[tile, :, start : start + SIDE] = jnp.where(hit, 1.0 / (CELL * CELL), 0.0).astype(BF16)


def put_corner_weights(weights, tile, start, lane, offset, low, high, exists):
    place = iota((1, LANES), 1)
    valid = (place >= low) & (place < high) & (place + offset < CELL)
    target = jnp.where(valid, lane, -1)
    target = jnp.where(exists > 0, target, -1)
    hit = iota((LANES, LANES), 0) == jnp.broadcast_to(target, (LANES, LANES))
    weights[tile, :, start : start + LANES] = jnp.where(hit, 1.0 / (CELL * CELL), 0.0).astype(BF16)


def folded(parts):
    parts = (parts[:ROWS] + parts[ROWS:]).reshape(KINDS, 8, parts.shape[-1])
    return jnp.broadcast_to(jnp.sum(parts, axis=1, keepdims=True), parts.shape)


def xx_kind(p, q):
    p, q = min(p, q), max(p, q)
    if p == 3:
        return 21
    if q == 3:
        return 6 + p
    return (0, 3, 5)[p] + q - p


def xy_kind(p, q):
    if p == 3 and q == 3:
        return 21
    if q == 3:
        return 6 + p
    if p == 3:
        return 18 + q
    return 9 + 3 * p + q


def pair_terms(mats, edges, below, above):
    lane = iota((8, LANES), 1)
    row = iota((8, LANES), 0)
    at_a = (lane & G) == 0
    total = jnp.zeros((32, LANES), F32)
    for q in range(4):
        rows = slice(8 * q, 8 * q + 8)
        own = edges[rows]
        other = roll(own, 4, 0)
        near = jnp.where(
            lane < G,
            roll(below[rows], -G, 1),
            jnp.where(
                lane < 2 * G,
                roll(above[rows], G, 1),
                jnp.where(lane < 3 * G, roll(other, -G, 1), roll(other, G, 1)),
            ),
        )
        moved = jnp.where(at_a, roll(near, -1, 1), roll(near, 1, 1))
        swapped = roll(near, 4, 0)
        corner = jnp.where(row < 4, roll(swapped, G - 1, 1), roll(swapped, 1 - G, 1))
        for kind, values in enumerate((own, near, moved, corner)):
            total = total + mats[kind, q] * jnp.concatenate([values] * 4, axis=0)
    return total


def by_colour(values):
    narrow = values[:, :LANES]
    for start in range(LANES, NODES, LANES):
        narrow = narrow + values[:, start : start + LANES]
    narrow = (narrow[0:8] + narrow[8:16]) + (narrow[16:24] + narrow[24:32])
    return jnp.sum(narrow + roll(narrow, 4, 0), axis=1, keepdims=True)


def per_row(values):
    return jnp.concatenate([values] * 4, axis=0)


def kernel(
    n,
    rows_ref,
    cols_ref,
    off_ref,
    ext_ref,
    prior_ref,
    x_ref,
    res_ref,
    below_ref,
    above_ref,
    head_ref,
    below_head,
    above_head,
    edge_ref,
    below_edge,
    above_edge,
    sums_ref,
    field_ref,
    lhs,
    weights,
    corner_lhs,
    corner_weights,
    mats,
    send_sem,
    recv_sem,
    sum_send,
    sum_recv,
):
    me = lax.axis_index("row")
    barrier = pltpu.get_barrier_semaphore()

    def greet(step, carry):
        pl.semaphore_signal(barrier, inc=1, device_id={"row": lax.rem(me + step, n)})
        return carry

    lax.fori_loop(1, n, greet, 0)

    has_below = jnp.where(me < n - 1, 1, 0)
    has_above = jnp.where(me > 0, 1, 0)

    field_ref[...] = jnp.zeros_like(field_ref)
    for tile in range(2):
        for colour in range(3):
            for p in range(4):
                spot = p * 8 + tile * 4 + colour
                field_ref[spot : spot + 1, :] = prior_ref[0, tile, colour, p : p + 1, :]
    row = iota((32, NODES), 0)
    unit = jnp.where(((row & 3) == (row >> 3)) & ((row & 3) < 3), 1.0, 0.0)
    rhs = 0.5 * (unit + field_ref[...])
    select = edge_matrix()
    edges = joined(dot_nt(thirds(rhs), select))
    head_ref[:META, :] = edges
    for tile in range(2):
        for direction in range(4):
            spot = META + tile * 12 + direction * 3
            numbers = (
                off_ref[0, tile, direction],
                ext_ref[0, tile, direction, 0],
                ext_ref[0, tile, direction, 1],
            )
            for which, number in enumerate(numbers):
                head_ref[spot + which : spot + which + 1, :] = jnp.full(
                    (1, LANES), number, jnp.int32
                ).astype(F32)

    pl.semaphore_wait(barrier, n - 1)

    def up(source, target, slot):
        return pltpu.make_async_remote_copy(
            src_ref=source,
            dst_ref=target,
            send_sem=send_sem.at[slot],
            recv_sem=recv_sem.at[slot],
            device_id={"row": lax.rem(me + n - 1, n)},
        )

    def down(source, target, slot):
        return pltpu.make_async_remote_copy(
            src_ref=source,
            dst_ref=target,
            send_sem=send_sem.at[slot],
            recv_sem=recv_sem.at[slot],
            device_id={"row": lax.rem(me + 1, n)},
        )

    def exchange(ups, downs, zeros_below, zeros_above):
        @pl.when(me > 0)
        def _():
            for copy in ups:
                copy.start()

        @pl.when(me < n - 1)
        def _():
            for copy in downs:
                copy.start()

        @pl.when(me == n - 1)
        def _():
            for ref in zeros_below:
                ref[...] = jnp.zeros_like(ref)

        @pl.when(me == 0)
        def _():
            for ref in zeros_above:
                ref[...] = jnp.zeros_like(ref)

    def arrive(ups, downs):
        @pl.when(me < n - 1)
        def _():
            for copy in ups:
                copy.wait_recv()

        @pl.when(me > 0)
        def _():
            for copy in downs:
                copy.wait_recv()

    def leave(ups, downs):
        @pl.when(me > 0)
        def _():
            for copy in ups:
                copy.wait_send()

        @pl.when(me < n - 1)
        def _():
            for copy in downs:
                copy.wait_send()

    ups = (up(rows_ref.at[0, :, 0], below_ref, 0), up(head_ref, below_head, 1))
    downs = (down(rows_ref.at[0, :, 1], above_ref, 2), down(head_ref, above_head, 3))
    exchange(ups, downs, (below_ref, below_head), (above_ref, above_head))

    offset = meta_row(head_ref, 0, 0, 0, SIDE)
    low = meta_row(head_ref, 0, 0, 1, SIDE)
    high = meta_row(head_ref, 0, 0, 2, SIDE)
    east_a = flat(cols_ref[0, 0, 1])
    east_b = aligned(flat(cols_ref[0, 1, 0]), offset)
    put_products(lhs, 0, 0, east_a, east_b)
    put_products(lhs, 1, 0, east_b, east_a)
    put_weights(weights, 0, 0, 2 * G, False, offset, low, high, 1)
    put_weights(weights, 1, 0, 3 * G, True, offset, low, high, 1)
    for tile in range(2):
        offset = meta_row(head_ref, tile, 1, 0, SIDE)
        low = meta_row(head_ref, tile, 1, 1, SIDE)
        high = meta_row(head_ref, tile, 1, 2, SIDE)
        put_weights(weights, tile, SIDE, 0, False, offset, low, high, has_below)
    image = smooth(rhs)

    arrive(ups, downs)
    last = slice(SIDE - LANES, SIDE)
    first = slice(0, LANES)
    for tile in range(2):
        offset = meta_row(head_ref, tile, 1, 0, SIDE)
        south_a = flat(rows_ref[0, tile, 1])
        south_b = aligned(flat(below_ref[tile]), offset)
        put_products(lhs, tile, SIDE, south_a, south_b)

        offset = meta_row(above_head, tile, 1, 0, SIDE)
        low = meta_row(above_head, tile, 1, 1, SIDE)
        high = meta_row(above_head, tile, 1, 2, SIDE)
        north_a = flat(above_ref[tile])
        north_b = aligned(flat(rows_ref[0, tile, 0]), offset)
        put_products(lhs, tile, 2 * SIDE, north_b, north_a)
        put_weights(weights, tile, 2 * SIDE, G, True, offset, low, high, has_above)

        direction = 2 + tile
        offset = meta_row(head_ref, tile, direction, 0, LANES)
        low = meta_row(head_ref, tile, direction, 1, LANES)
        high = meta_row(head_ref, tile, direction, 2, LANES)
        if tile == 0:
            corner_a = roll(flat(rows_ref[0, 0, 1, :, :, last]), CELL, 1)
            corner_b = flat(below_ref[1, :, :, first])
        else:
            corner_a = flat(rows_ref[0, 1, 1, :, :, first])
            corner_b = roll(flat(below_ref[0, :, :, last]), CELL, 1)
        put_products(corner_lhs, tile, 0, corner_a, aligned(corner_b, offset))
        spot = G - 1 if tile == 0 else 0
        put_corner_weights(corner_weights, tile, 0, spot, offset, low, high, has_below)

        direction = 3 - tile
        offset = meta_row(above_head, 1 - tile, direction, 0, LANES)
        low = meta_row(above_head, 1 - tile, direction, 1, LANES)
        high = meta_row(above_head, 1 - tile, direction, 2, LANES)
        if tile == 0:
            corner_a = flat(above_ref[1, :, :, first])
            corner_b = roll(flat(rows_ref[0, 0, 0, :, :, last]), CELL, 1)
        else:
            corner_a = roll(flat(above_ref[0, :, :, last]), CELL, 1)
            corner_b = flat(rows_ref[0, 1, 0, :, :, first])
        put_products(corner_lhs, tile, LANES, aligned(corner_b, offset), corner_a)
        spot = 2 * G - 1 if tile == 0 else G
        put_corner_weights(corner_weights, tile, LANES, spot, offset, low, high, has_above)

    plain = [folded(dot_nt(lhs[tile], weights[tile])) for tile in range(2)]
    extra = [folded(dot_nt(corner_lhs[tile], corner_weights[tile])) for tile in range(2)]
    top = iota((KINDS, 8, LANES), 1) < 4
    none = jnp.where(top, plain[0][..., :LANES], plain[1][..., :LANES])
    one = jnp.where(top, plain[0][..., LANES:], plain[1][..., LANES:])
    corner = jnp.where(top, extra[0], extra[1])
    whole = none + one + corner
    for q in range(4):
        for kind, values, index in (
            (0, whole, xx_kind),
            (1, -none, xy_kind),
            (2, -one, xy_kind),
            (3, -corner, xy_kind),
        ):
            mats[kind, q] = jnp.concatenate([values[index(p, q)] for p in range(4)], axis=0)

    terms = pair_terms(mats, edges, below_head[:META, :], above_head[:META, :])
    image = image + joined(dot_nn(thirds(terms), select))
    edges = joined(dot_nt(thirds(image), select))
    edge_ref[...] = edges
    ups_edge = (up(edge_ref, below_edge, 4),)
    downs_edge = (down(edge_ref, above_edge, 5),)
    exchange(ups_edge, downs_edge, (below_edge,), (above_edge,))

    lane8 = iota((8, LANES), 1)

    def packed(values):
        total = jnp.zeros((8, LANES), F32)
        for spot, value in enumerate(values):
            total = jnp.where(lane8 == spot, value, total)
        return total

    def sum_copy(phase, step, owner):
        return pltpu.make_async_remote_copy(
            src_ref=sums_ref.at[phase, me],
            dst_ref=sums_ref.at[phase, owner],
            send_sem=sum_send.at[phase, step],
            recv_sem=sum_recv.at[phase, step],
            device_id={"row": lax.rem(me + step, n)},
        )

    def sums_start(phase, values):
        sums_ref[phase, me] = values

        def send(step, carry):
            sum_copy(phase, step, me).start()
            return carry

        lax.fori_loop(1, n, send, 0)

    def sums_end(phase):
        def receive(step, carry):
            sum_copy(phase, step, lax.rem(me + n - step, n)).wait_recv()
            return carry

        lax.fori_loop(1, n, receive, 0)
        return jnp.sum(sums_ref[phase], axis=0)

    sums_start(0, packed((by_colour(rhs * rhs), by_colour(rhs * image))))

    second = smooth(image)
    arrive(ups_edge, downs_edge)
    terms = pair_terms(mats, edges, below_edge[...], above_edge[...])
    second = second + joined(dot_nn(thirds(terms), select))

    real = (iota((8, 1), 0) & 3) < 3
    sums = sums_end(0)
    norm = jnp.where(real, sums[:, 0:1], 1.0)
    curvature = jnp.where(real, sums[:, 1:2], 1.0)
    alpha = norm / curvature
    step = per_row(alpha)
    residual = rhs - step * image
    lifted = image - step * second
    sums_start(
        1,
        packed(
            (
                by_colour(residual * residual),
                by_colour(residual * lifted),
                by_colour(residual * image),
            )
        ),
    )
    sums = sums_end(1)
    norm_next = jnp.where(real, sums[:, 0:1], 1.0)
    beta = norm_next / norm
    bend = sums[:, 1:2] + 2.0 * beta * sums[:, 2:3] + beta * beta * curvature
    alpha_next = norm_next / jnp.where(real, bend, 1.0)
    turn = per_row(beta)
    step_next = per_row(alpha_next)
    answer = step * rhs + step_next * (residual + turn * rhs)
    left = residual - step_next * (lifted + turn * image)
    for tile in range(2):
        for colour in range(3):
            for p in range(4):
                spot = p * 8 + tile * 4 + colour
                x_ref[0, tile, colour, p : p + 1, :] = answer[spot : spot + 1]
                res_ref[0, tile, colour, p : p + 1, :] = left[spot : spot + 1]

    leave(ups, downs)
    leave(ups_edge, downs_edge)

    def sent(step, carry):
        sum_copy(0, step, me).wait_send()
        sum_copy(1, step, me).wait_send()
        return carry

    lax.fori_loop(1, n, sent, 0)


def on_device(n, rows_strip, cols_strip, offsets, extents, prior):
    vmem = pl.BlockSpec(memory_space=pltpu.VMEM)
    smem = pl.BlockSpec(memory_space=pltpu.SMEM)
    shape = jax.ShapeDtypeStruct(prior.shape, F32)
    margins = rows_strip.shape[1:2] + rows_strip.shape[3:]
    return pl.pallas_call(
        functools.partial(kernel, n),
        out_shape=(shape, shape),
        in_specs=[vmem, vmem, smem, smem, vmem],
        out_specs=(vmem, vmem),
        scratch_shapes=[
            pltpu.VMEM(margins, BF16),
            pltpu.VMEM(margins, BF16),
            pltpu.VMEM((META + 24, LANES), F32),
            pltpu.VMEM((META + 24, LANES), F32),
            pltpu.VMEM((META + 24, LANES), F32),
            pltpu.VMEM((META, LANES), F32),
            pltpu.VMEM((META, LANES), F32),
            pltpu.VMEM((META, LANES), F32),
            pltpu.VMEM((2, n, 8, LANES), F32),
            pltpu.VMEM((32, NODES), F32),
            pltpu.VMEM((2, 2 * ROWS, 3 * SIDE), BF16),
            pltpu.VMEM((2, 2 * LANES, 3 * SIDE), BF16),
            pltpu.VMEM((2, 2 * ROWS, 2 * LANES), BF16),
            pltpu.VMEM((2, LANES, 2 * LANES), BF16),
            pltpu.VMEM((4, 4, 32, LANES), F32),
            pltpu.SemaphoreType.DMA((6,)),
            pltpu.SemaphoreType.DMA((6,)),
            pltpu.SemaphoreType.DMA((2, n)),
            pltpu.SemaphoreType.DMA((2, n)),
        ],
        compiler_params=pltpu.CompilerParams(
            collective_id=0, has_side_effects=True, vmem_limit_bytes=48 * 1024 * 1024
        ),
    )(rows_strip, cols_strip, offsets, extents, prior)


def solution(mesh):
    return jax.shard_map(
        functools.partial(on_device, mesh.shape["row"]),
        mesh=mesh,
        in_specs=(
            P(("slab", "row"), None, None, None, None, None),
            P(("slab", "row"), None, None, None, None, None),
            P(("slab", "row"), None, None),
            P(("slab", "row"), None, None, None),
            P(("slab", "row"), None, None, None, None),
        ),
        out_specs=(
            P(("slab", "row"), None, None, None, None),
            P(("slab", "row"), None, None, None, None),
        ),
        check_vma=False,
    )
```

```python
import functools

import jax
import jax.numpy as jnp
from jax import lax
from jax.experimental import pallas as pl
from jax.experimental.pallas import tpu as pltpu
from jax.sharding import PartitionSpec as P

G = 32
CELL = 16
NODES = G * G
SIDE = G * CELL
LANES = 128
KINDS = 22
ROWS = KINDS * 8
META = 32

F32 = jnp.float32
BF16 = jnp.bfloat16


def iota(shape, axis):
    return lax.broadcasted_iota(jnp.int32, shape, axis)


def roll(values, shift, axis):
    return pltpu.roll(values, shift % values.shape[axis], axis)


def dot_nt(first, second):
    return lax.dot_general(first, second, (((1,), (1,)), ((), ())), preferred_element_type=F32)


def dot_nn(first, second):
    return lax.dot_general(first, second, (((1,), (0,)), ((), ())), preferred_element_type=F32)


def thirds(values):
    high = values.astype(BF16)
    rest = values - high.astype(F32)
    middle = rest.astype(BF16)
    low = (rest - middle.astype(F32)).astype(BF16)
    return jnp.concatenate([high, middle, low], axis=0)


def joined(parts):
    size = parts.shape[0] // 3
    return parts[:size] + (parts[size : 2 * size] + parts[2 * size :])


def edge_matrix():
    lane = iota((LANES, NODES), 0)
    node = iota((LANES, NODES), 1)
    spot = lane & (G - 1)
    target = jnp.where(
        lane < G,
        NODES - G + spot,
        jnp.where(lane < 2 * G, spot, jnp.where(lane < 3 * G, spot * G + G - 1, spot * G)),
    )
    return jnp.where(node == target, 1.0, 0.0).astype(BF16)


def smooth(field):
    node = iota((1, NODES), 1)
    column = node & (G - 1)
    up = jnp.where(node >= G, 1.0, 0.0)
    down = jnp.where(node < NODES - G, 1.0, 0.0)
    left = jnp.where(column > 0, 1.0, 0.0)
    right = jnp.where(column < G - 1, 1.0, 0.0)
    total = (0.5 + up + down + left + right) * field
    total = total - up * roll(field, G, 1) - down * roll(field, -G, 1)
    return total - left * roll(field, 1, 1) - right * roll(field, -1, 1)


def meta_row(buffer, tile, direction, which, width):
    spot = META + tile * 12 + direction * 3 + which
    row = buffer[spot : spot + 1, :].astype(jnp.int32)
    return jnp.concatenate([row] * (width // LANES), axis=1)


def aligned(strip, offset):
    amount = jnp.broadcast_to(offset, strip.shape)
    for bit in range(4):
        strip = jnp.where((amount & (1 << bit)) != 0, roll(strip, -(1 << bit), 1), strip)
    return strip


def flat(strip):
    return strip.astype(F32).reshape(3 * CELL, strip.shape[-1])


def put_products(lhs, tile, start, x, y):
    width = x.shape[-1]
    x = x.reshape(3, CELL, width)
    y = y.reshape(3, CELL, width)
    products = jnp.concatenate(
        [
            x[0:1] * x,
            x[1:2] * x[1:],
            x[2:3] * x[2:],
            x,
            x[0:1] * y,
            x[1:2] * y,
            x[2:3] * y,
            y,
            jnp.ones((1, CELL, width), F32),
        ],
        axis=0,
    )
    sums = (products[:, :8] + products[:, 8:]).reshape(ROWS, width)
    high = sums.astype(BF16)
    lhs[tile, :ROWS, start : start + width] = high
    lhs[tile, ROWS:, start : start + width] = (sums - high.astype(F32)).astype(BF16)


def put_weights(weights, tile, start, base, at_b, offset, low, high, exists):
    place = iota((1, SIDE), 1)
    moved = place + offset
    valid = (place >= low) & (place < high) & (moved < SIDE)
    split = (moved >> 4) - (place >> 4)
    cell = (moved >> 4) if at_b else (place >> 4)
    target = jnp.where(valid, base + cell + LANES * split, -1)
    target = jnp.where(exists > 0, target, -1)
    hit = iota((2 * LANES, SIDE), 0) == jnp.broadcast_to(target, (2 * LANES, SIDE))
    weights[tile, :, start : start + SIDE] = jnp.where(hit, 1.0 / (CELL * CELL), 0.0).astype(BF16)


def put_corner_weights(weights, tile, start, lane, offset, low, high, exists):
    place = iota((1, LANES), 1)
    valid = (place >= low) & (place < high) & (place + offset < CELL)
    target = jnp.where(valid, lane, -1)
    target = jnp.where(exists > 0, target, -1)
    hit = iota((LANES, LANES), 0) == jnp.broadcast_to(target, (LANES, LANES))
    weights[tile, :, start : start + LANES] = jnp.where(hit, 1.0 / (CELL * CELL), 0.0).astype(BF16)


def folded(parts):
    parts = (parts[:ROWS] + parts[ROWS:]).reshape(KINDS, 8, parts.shape[-1])
    return jnp.broadcast_to(jnp.sum(parts, axis=1, keepdims=True), parts.shape)


def xx_kind(p, q):
    p, q = min(p, q), max(p, q)
    if p == 3:
        return 21
    if q == 3:
        return 6 + p
    return (0, 3, 5)[p] + q - p


def xy_kind(p, q):
    if p == 3 and q == 3:
        return 21
    if q == 3:
        return 6 + p
    if p == 3:
        return 18 + q
    return 9 + 3 * p + q


def pair_terms(mats, edges, below, above):
    lane = iota((8, LANES), 1)
    row = iota((8, LANES), 0)
    at_a = (lane & G) == 0
    total = jnp.zeros((32, LANES), F32)
    for q in range(4):
        rows = slice(8 * q, 8 * q + 8)
        own = edges[rows]
        other = roll(own, 4, 0)
        near = jnp.where(
            lane < G,
            roll(below[rows], -G, 1),
            jnp.where(
                lane < 2 * G,
                roll(above[rows], G, 1),
                jnp.where(lane < 3 * G, roll(other, -G, 1), roll(other, G, 1)),
            ),
        )
        moved = jnp.where(at_a, roll(near, -1, 1), roll(near, 1, 1))
        swapped = roll(near, 4, 0)
        corner = jnp.where(row < 4, roll(swapped, G - 1, 1), roll(swapped, 1 - G, 1))
        for kind, values in enumerate((own, near, moved, corner)):
            total = total + mats[kind, q] * jnp.concatenate([values] * 4, axis=0)
    return total


def by_colour(values):
    narrow = values[:, :LANES]
    for start in range(LANES, NODES, LANES):
        narrow = narrow + values[:, start : start + LANES]
    narrow = (narrow[0:8] + narrow[8:16]) + (narrow[16:24] + narrow[24:32])
    return jnp.sum(narrow + roll(narrow, 4, 0), axis=1, keepdims=True)


def per_row(values):
    return jnp.concatenate([values] * 4, axis=0)


def kernel(
    n,
    rows_ref,
    cols_ref,
    off_ref,
    ext_ref,
    prior_ref,
    x_ref,
    res_ref,
    below_ref,
    above_ref,
    head_ref,
    below_head,
    above_head,
    edge_ref,
    below_edge,
    above_edge,
    sums_ref,
    rows_here,
    east_near,
    east_far,
    prior_here,
    field_ref,
    lhs,
    weights,
    corner_lhs,
    corner_weights,
    mats,
    send_sem,
    recv_sem,
    sum_send,
    sum_recv,
    load_sem,
):
    me = lax.axis_index("row")
    barrier = pltpu.get_barrier_semaphore()

    def greet(step, carry):
        pl.semaphore_signal(barrier, inc=1, device_id={"row": lax.rem(me + step, n)})
        return carry

    lax.fori_loop(1, n, greet, 0)

    loads = [
        pltpu.make_async_copy(source, target, load_sem.at[slot])
        for slot, (source, target) in enumerate(
            (
                (prior_ref.at[0], prior_here),
                (cols_ref.at[0, 0, 1], east_near),
                (cols_ref.at[0, 1, 0], east_far),
                (rows_ref.at[0], rows_here),
            )
        )
    ]
    for load in loads:
        load.start()

    has_below = jnp.where(me < n - 1, 1, 0)
    has_above = jnp.where(me > 0, 1, 0)

    def up(source, target, slot):
        return pltpu.make_async_remote_copy(
            src_ref=source,
            dst_ref=target,
            send_sem=send_sem.at[slot],
            recv_sem=recv_sem.at[slot],
            device_id={"row": lax.rem(me + n - 1, n)},
        )

    def down(source, target, slot):
        return pltpu.make_async_remote_copy(
            src_ref=source,
            dst_ref=target,
            send_sem=send_sem.at[slot],
            recv_sem=recv_sem.at[slot],
            device_id={"row": lax.rem(me + 1, n)},
        )

    def exchange(ups, downs, zeros_below, zeros_above):
        @pl.when(me > 0)
        def _():
            for copy in ups:
                copy.start()

        @pl.when(me < n - 1)
        def _():
            for copy in downs:
                copy.start()

        @pl.when(me == n - 1)
        def _():
            for ref in zeros_below:
                ref[...] = jnp.zeros_like(ref)

        @pl.when(me == 0)
        def _():
            for ref in zeros_above:
                ref[...] = jnp.zeros_like(ref)

    def arrive(ups, downs):
        @pl.when(me < n - 1)
        def _():
            for copy in ups:
                copy.wait_recv()

        @pl.when(me > 0)
        def _():
            for copy in downs:
                copy.wait_recv()

    def leave(ups, downs):
        @pl.when(me > 0)
        def _():
            for copy in ups:
                copy.wait_send()

        @pl.when(me < n - 1)
        def _():
            for copy in downs:
                copy.wait_send()

    select = edge_matrix()
    field_ref[...] = jnp.zeros_like(field_ref)
    pl.semaphore_wait(barrier, n - 1)
    ups_wide = (up(rows_ref.at[0, :, 0], below_ref, 0),)
    downs_wide = (down(rows_ref.at[0, :, 1], above_ref, 2),)
    exchange(ups_wide, downs_wide, (below_ref,), (above_ref,))

    loads[0].wait()
    for tile in range(2):
        for colour in range(3):
            for p in range(4):
                spot = p * 8 + tile * 4 + colour
                field_ref[spot : spot + 1, :] = prior_here[tile, colour, p : p + 1, :]
    row = iota((32, NODES), 0)
    unit = jnp.where(((row & 3) == (row >> 3)) & ((row & 3) < 3), 1.0, 0.0)
    rhs = 0.5 * (unit + field_ref[...])
    edges = joined(dot_nt(thirds(rhs), select))
    head_ref[:META, :] = edges
    for tile in range(2):
        for direction in range(4):
            spot = META + tile * 12 + direction * 3
            numbers = (
                off_ref[0, tile, direction],
                ext_ref[0, tile, 0, direction],
                ext_ref[0, tile, 1, direction],
            )
            for which, number in enumerate(numbers):
                head_ref[spot + which : spot + which + 1, :] = jnp.full(
                    (1, LANES), number, jnp.int32
                ).astype(F32)

    ups = (up(head_ref, below_head, 1),)
    downs = (down(head_ref, above_head, 3),)
    exchange(ups, downs, (below_head,), (above_head,))
    ups = ups + ups_wide
    downs = downs + downs_wide

    offset = meta_row(head_ref, 0, 0, 0, SIDE)
    low = meta_row(head_ref, 0, 0, 1, SIDE)
    high = meta_row(head_ref, 0, 0, 2, SIDE)
    loads[1].wait()
    loads[2].wait()
    east_a = flat(east_near[...])
    east_b = aligned(flat(east_far[...]), offset)
    put_products(lhs, 0, 0, east_a, east_b)
    put_products(lhs, 1, 0, east_b, east_a)
    put_weights(weights, 0, 0, 2 * G, False, offset, low, high, 1)
    put_weights(weights, 1, 0, 3 * G, True, offset, low, high, 1)
    for tile in range(2):
        offset = meta_row(head_ref, tile, 1, 0, SIDE)
        low = meta_row(head_ref, tile, 1, 1, SIDE)
        high = meta_row(head_ref, tile, 1, 2, SIDE)
        put_weights(weights, tile, SIDE, 0, False, offset, low, high, has_below)
    image = smooth(rhs)

    loads[3].wait()
    arrive(ups, downs)
    last = slice(SIDE - LANES, SIDE)
    first = slice(0, LANES)
    for tile in range(2):
        offset = meta_row(head_ref, tile, 1, 0, SIDE)
        south_a = flat(rows_here[tile, 1])
        south_b = aligned(flat(below_ref[tile]), offset)
        put_products(lhs, tile, SIDE, south_a, south_b)

        offset = meta_row(above_head, tile, 1, 0, SIDE)
        low = meta_row(above_head, tile, 1, 1, SIDE)
        high = meta_row(above_head, tile, 1, 2, SIDE)
        north_a = flat(above_ref[tile])
        north_b = aligned(flat(rows_here[tile, 0]), offset)
        put_products(lhs, tile, 2 * SIDE, north_b, north_a)
        put_weights(weights, tile, 2 * SIDE, G, True, offset, low, high, has_above)

        direction = 2 + tile
        offset = meta_row(head_ref, tile, direction, 0, LANES)
        low = meta_row(head_ref, tile, direction, 1, LANES)
        high = meta_row(head_ref, tile, direction, 2, LANES)
        if tile == 0:
            corner_a = roll(flat(rows_here[0, 1, :, :, last]), CELL, 1)
            corner_b = flat(below_ref[1, :, :, first])
        else:
            corner_a = flat(rows_here[1, 1, :, :, first])
            corner_b = roll(flat(below_ref[0, :, :, last]), CELL, 1)
        put_products(corner_lhs, tile, 0, corner_a, aligned(corner_b, offset))
        spot = G - 1 if tile == 0 else 0
        put_corner_weights(corner_weights, tile, 0, spot, offset, low, high, has_below)

        direction = 3 - tile
        offset = meta_row(above_head, 1 - tile, direction, 0, LANES)
        low = meta_row(above_head, 1 - tile, direction, 1, LANES)
        high = meta_row(above_head, 1 - tile, direction, 2, LANES)
        if tile == 0:
            corner_a = flat(above_ref[1, :, :, first])
            corner_b = roll(flat(rows_here[0, 0, :, :, last]), CELL, 1)
        else:
            corner_a = roll(flat(above_ref[0, :, :, last]), CELL, 1)
            corner_b = flat(rows_here[1, 0, :, :, first])
        put_products(corner_lhs, tile, LANES, aligned(corner_b, offset), corner_a)
        spot = 2 * G - 1 if tile == 0 else G
        put_corner_weights(corner_weights, tile, LANES, spot, offset, low, high, has_above)

    plain = [folded(dot_nt(lhs[tile], weights[tile])) for tile in range(2)]
    extra = [folded(dot_nt(corner_lhs[tile], corner_weights[tile])) for tile in range(2)]
    top = iota((KINDS, 8, LANES), 1) < 4
    none = jnp.where(top, plain[0][..., :LANES], plain[1][..., :LANES])
    one = jnp.where(top, plain[0][..., LANES:], plain[1][..., LANES:])
    corner = jnp.where(top, extra[0], extra[1])
    whole = none + one + corner
    for q in range(4):
        for kind, values, index in (
            (0, whole, xx_kind),
            (1, -none, xy_kind),
            (2, -one, xy_kind),
            (3, -corner, xy_kind),
        ):
            mats[kind, q] = jnp.concatenate([values[index(p, q)] for p in range(4)], axis=0)

    terms = pair_terms(mats, edges, below_head[:META, :], above_head[:META, :])
    image = image + joined(dot_nn(thirds(terms), select))
    edges = joined(dot_nt(thirds(image), select))
    edge_ref[...] = edges
    ups_edge = (up(edge_ref, below_edge, 4),)
    downs_edge = (down(edge_ref, above_edge, 5),)
    exchange(ups_edge, downs_edge, (below_edge,), (above_edge,))

    lane = iota((8, LANES), 1)
    row = iota((8, LANES), 0)
    spread = (lane == (row & 3)) & (lane < 3)

    def as_row(column):
        return jnp.sum(jnp.where(spread & (row < 4), column, 0.0), axis=0, keepdims=True)

    def as_column(values):
        column = jnp.sum(jnp.where(spread, values, 0.0), axis=1, keepdims=True)
        return jnp.concatenate([column] * 4, axis=0)

    rr = by_colour(rhs * rhs)
    rq = by_colour(rhs * image)
    theta = jnp.clip(jnp.where(rr > 0.0, rq / jnp.where(rr > 0.0, rr, 1.0), 0.0), 0.0, 20.0)
    tilt = per_row(theta)
    bent = image - tilt * rhs
    ru = by_colour(rhs * bent)
    uu = by_colour(bent * bent)

    second = smooth(image)
    arrive(ups_edge, downs_edge)
    terms = pair_terms(mats, edges, below_edge[...], above_edge[...])
    second = second + joined(dot_nn(thirds(terms), select))
    twice = second - tilt * image
    rv = by_colour(rhs * twice)
    uv = by_colour(bent * twice)
    parts = [as_row(value) for value in (rr, rq, ru, uu, rv, uv, theta)]
    sums_ref[me] = jnp.concatenate(parts + [jnp.zeros((1, LANES), F32)], axis=0)

    def sum_copy(step, owner):
        return pltpu.make_async_remote_copy(
            src_ref=sums_ref.at[me],
            dst_ref=sums_ref.at[owner],
            send_sem=sum_send.at[step],
            recv_sem=sum_recv.at[step],
            device_id={"row": lax.rem(me + step, n)},
        )

    def send(step, carry):
        sum_copy(step, me).start()
        return carry

    def receive(step, carry):
        sum_copy(step, lax.rem(me + n - step, n)).wait_recv()
        return carry

    lax.fori_loop(1, n, send, 0)
    lax.fori_loop(1, n, receive, 0)
    rr, rq, ru, uu, rv, uv, theta = [sums_ref[:, spot, :] for spot in range(7)]

    def total(values):
        return jnp.sum(values, axis=0, keepdims=True)

    real = iota((1, LANES), 1) < 3
    norm = jnp.where(real, total(rr), 1.0)
    curvature = jnp.where(real, total(rq), 1.0)
    alpha = norm / curvature
    keep = 1.0 - alpha * theta
    uq = uu + theta * ru
    norm_next = total(keep * keep * rr - 2.0 * alpha * keep * ru + alpha * alpha * uu)
    with_image = total(keep * rq - alpha * uq)
    with_lifted = total(keep * keep * rq - alpha * keep * (rv + uq) + alpha * alpha * uv)
    beta = norm_next / norm
    bend = with_lifted + 2.0 * beta * with_image + beta * beta * curvature
    alpha_next = norm_next / jnp.where(real, bend, 1.0)
    step = as_column(alpha)
    step_next = as_column(alpha_next)
    turn = as_column(beta)
    residual = rhs - step * image
    lifted = image - step * second
    answer = step * rhs + step_next * (residual + turn * rhs)
    left = residual - step_next * (lifted + turn * image)
    for tile in range(2):
        for colour in range(3):
            for p in range(4):
                spot = p * 8 + tile * 4 + colour
                x_ref[0, tile, colour, p : p + 1, :] = answer[spot : spot + 1]
                res_ref[0, tile, colour, p : p + 1, :] = left[spot : spot + 1]

    leave(ups, downs)
    leave(ups_edge, downs_edge)

    def sent(step, carry):
        sum_copy(step, me).wait_send()
        return carry

    lax.fori_loop(1, n, sent, 0)


def on_device(n, rows_strip, cols_strip, offsets, extents, prior):
    vmem = pl.BlockSpec(memory_space=pltpu.VMEM)
    hbm = pl.BlockSpec(memory_space=pltpu.HBM)
    smem = pl.BlockSpec(memory_space=pltpu.SMEM)
    shape = jax.ShapeDtypeStruct(prior.shape, F32)
    margins = rows_strip.shape[1:2] + rows_strip.shape[3:]
    return pl.pallas_call(
        functools.partial(kernel, n),
        out_shape=(shape, shape),
        in_specs=[hbm, hbm, smem, smem, hbm],
        out_specs=(vmem, vmem),
        scratch_shapes=[
            pltpu.VMEM(margins, BF16),
            pltpu.VMEM(margins, BF16),
            pltpu.VMEM((META + 24, LANES), F32),
            pltpu.VMEM((META + 24, LANES), F32),
            pltpu.VMEM((META + 24, LANES), F32),
            pltpu.VMEM((META, LANES), F32),
            pltpu.VMEM((META, LANES), F32),
            pltpu.VMEM((META, LANES), F32),
            pltpu.VMEM((n, 8, LANES), F32),
            pltpu.VMEM(rows_strip.shape[1:], BF16),
            pltpu.VMEM(cols_strip.shape[3:], BF16),
            pltpu.VMEM(cols_strip.shape[3:], BF16),
            pltpu.VMEM(prior.shape[1:], F32),
            pltpu.VMEM((32, NODES), F32),
            pltpu.VMEM((2, 2 * ROWS, 3 * SIDE), BF16),
            pltpu.VMEM((2, 2 * LANES, 3 * SIDE), BF16),
            pltpu.VMEM((2, 2 * ROWS, 2 * LANES), BF16),
            pltpu.VMEM((2, LANES, 2 * LANES), BF16),
            pltpu.VMEM((4, 4, 32, LANES), F32),
            pltpu.SemaphoreType.DMA((6,)),
            pltpu.SemaphoreType.DMA((6,)),
            pltpu.SemaphoreType.DMA((n,)),
            pltpu.SemaphoreType.DMA((n,)),
            pltpu.SemaphoreType.DMA((4,)),
        ],
        compiler_params=pltpu.CompilerParams(
            collective_id=0, has_side_effects=True, vmem_limit_bytes=48 * 1024 * 1024
        ),
    )(rows_strip, cols_strip, offsets, extents.swapaxes(2, 3), prior)


def solution(mesh):
    return jax.shard_map(
        functools.partial(on_device, mesh.shape["row"]),
        mesh=mesh,
        in_specs=(
            P(("slab", "row"), None, None, None, None, None),
            P(("slab", "row"), None, None, None, None, None),
            P(("slab", "row"), None, None),
            P(("slab", "row"), None, None, None),
            P(("slab", "row"), None, None, None, None),
        ),
        out_specs=(
            P(("slab", "row"), None, None, None, None),
            P(("slab", "row"), None, None, None, None),
        ),
        check_vma=False,
    )
```

```python
import functools

import jax
import jax.numpy as jnp
from jax import lax
from jax.experimental import pallas as pl
from jax.experimental.pallas import tpu as pltpu
from jax.sharding import PartitionSpec as P

G = 32
CELL = 16
NODES = G * G
SIDE = G * CELL
LANES = 128
KINDS = 22
ROWS = KINDS * 8
META = 32

F32 = jnp.float32
BF16 = jnp.bfloat16


def iota(shape, axis):
    return lax.broadcasted_iota(jnp.int32, shape, axis)


def roll(values, shift, axis):
    return pltpu.roll(values, shift % values.shape[axis], axis)


def dot_nt(first, second):
    return lax.dot_general(first, second, (((1,), (1,)), ((), ())), preferred_element_type=F32)


def dot_nn(first, second):
    return lax.dot_general(first, second, (((1,), (0,)), ((), ())), preferred_element_type=F32)


def thirds(values):
    high = values.astype(BF16)
    rest = values - high.astype(F32)
    middle = rest.astype(BF16)
    low = (rest - middle.astype(F32)).astype(BF16)
    return jnp.concatenate([high, middle, low], axis=0)


def joined(parts):
    size = parts.shape[0] // 3
    return parts[:size] + (parts[size : 2 * size] + parts[2 * size :])


def edge_matrix():
    lane = iota((LANES, NODES), 0)
    node = iota((LANES, NODES), 1)
    spot = lane & (G - 1)
    target = jnp.where(
        lane < G,
        NODES - G + spot,
        jnp.where(lane < 2 * G, spot, jnp.where(lane < 3 * G, spot * G + G - 1, spot * G)),
    )
    return jnp.where(node == target, 1.0, 0.0).astype(BF16)


def smooth(field):
    node = iota((1, NODES), 1)
    column = node & (G - 1)
    up = jnp.where(node >= G, 1.0, 0.0)
    down = jnp.where(node < NODES - G, 1.0, 0.0)
    left = jnp.where(column > 0, 1.0, 0.0)
    right = jnp.where(column < G - 1, 1.0, 0.0)
    total = (0.5 + up + down + left + right) * field
    total = total - up * roll(field, G, 1) - down * roll(field, -G, 1)
    return total - left * roll(field, 1, 1) - right * roll(field, -1, 1)


def meta_row(buffer, tile, direction, which, width):
    spot = META + tile * 12 + direction * 3 + which
    row = buffer[spot : spot + 1, :].astype(jnp.int32)
    return jnp.concatenate([row] * (width // LANES), axis=1)


def aligned(strip, offset):
    amount = jnp.broadcast_to(offset, strip.shape)
    for bit in range(4):
        strip = jnp.where((amount & (1 << bit)) != 0, roll(strip, -(1 << bit), 1), strip)
    return strip


def flat(strip):
    return strip.astype(F32).reshape(3 * CELL, strip.shape[-1])


def put_products(lhs, tile, start, x, y):
    width = x.shape[-1]
    x = x.reshape(3, CELL, width)
    y = y.reshape(3, CELL, width)
    products = jnp.concatenate(
        [
            x[0:1] * x,
            x[1:2] * x[1:],
            x[2:3] * x[2:],
            x,
            x[0:1] * y,
            x[1:2] * y,
            x[2:3] * y,
            y,
            jnp.ones((1, CELL, width), F32),
        ],
        axis=0,
    )
    sums = (products[:, :8] + products[:, 8:]).reshape(ROWS, width)
    high = sums.astype(BF16)
    lhs[tile, :ROWS, start : start + width] = high
    lhs[tile, ROWS:, start : start + width] = (sums - high.astype(F32)).astype(BF16)


def put_weights(weights, tile, start, base, at_b, offset, low, high, exists):
    place = iota((1, SIDE), 1)
    moved = place + offset
    valid = (place >= low) & (place < high) & (moved < SIDE)
    split = (moved >> 4) - (place >> 4)
    cell = (moved >> 4) if at_b else (place >> 4)
    target = jnp.where(valid, base + cell + LANES * split, -1)
    target = jnp.where(exists > 0, target, -1)
    hit = iota((2 * LANES, SIDE), 0) == jnp.broadcast_to(target, (2 * LANES, SIDE))
    weights[tile, :, start : start + SIDE] = jnp.where(hit, 1.0 / (CELL * CELL), 0.0).astype(BF16)


def put_corner_weights(weights, tile, start, lane, offset, low, high, exists):
    place = iota((1, LANES), 1)
    valid = (place >= low) & (place < high) & (place + offset < CELL)
    target = jnp.where(valid, lane, -1)
    target = jnp.where(exists > 0, target, -1)
    hit = iota((LANES, LANES), 0) == jnp.broadcast_to(target, (LANES, LANES))
    weights[tile, :, start : start + LANES] = jnp.where(hit, 1.0 / (CELL * CELL), 0.0).astype(BF16)


def folded(parts):
    parts = (parts[:ROWS] + parts[ROWS:]).reshape(KINDS, 8, parts.shape[-1])
    return jnp.broadcast_to(jnp.sum(parts, axis=1, keepdims=True), parts.shape)


def xx_kind(p, q):
    p, q = min(p, q), max(p, q)
    if p == 3:
        return 21
    if q == 3:
        return 6 + p
    return (0, 3, 5)[p] + q - p


def xy_kind(p, q):
    if p == 3 and q == 3:
        return 21
    if q == 3:
        return 6 + p
    if p == 3:
        return 18 + q
    return 9 + 3 * p + q


def pair_terms(mats, edges, below, above):
    lane = iota((8, LANES), 1)
    row = iota((8, LANES), 0)
    at_a = (lane & G) == 0
    total = jnp.zeros((32, LANES), F32)
    for q in range(4):
        rows = slice(8 * q, 8 * q + 8)
        own = edges[rows]
        other = roll(own, 4, 0)
        near = jnp.where(
            lane < G,
            roll(below[rows], -G, 1),
            jnp.where(
                lane < 2 * G,
                roll(above[rows], G, 1),
                jnp.where(lane < 3 * G, roll(other, -G, 1), roll(other, G, 1)),
            ),
        )
        moved = jnp.where(at_a, roll(near, -1, 1), roll(near, 1, 1))
        swapped = roll(near, 4, 0)
        corner = jnp.where(row < 4, roll(swapped, G - 1, 1), roll(swapped, 1 - G, 1))
        for kind, values in enumerate((own, near, moved, corner)):
            total = total + mats[kind, q] * jnp.concatenate([values] * 4, axis=0)
    return total


def by_colour(values):
    narrow = values[:, :LANES]
    for start in range(LANES, NODES, LANES):
        narrow = narrow + values[:, start : start + LANES]
    narrow = (narrow[0:8] + narrow[8:16]) + (narrow[16:24] + narrow[24:32])
    return jnp.sum(narrow + roll(narrow, 4, 0), axis=1, keepdims=True)


def per_row(values):
    return jnp.concatenate([values] * 4, axis=0)


def kernel(
    n,
    rows_ref,
    cols_ref,
    off_ref,
    ext_ref,
    prior_ref,
    x_ref,
    res_ref,
    below_ref,
    above_ref,
    head_ref,
    below_head,
    above_head,
    edge_ref,
    below_edge,
    above_edge,
    sums_ref,
    rows_here,
    east_near,
    east_far,
    prior_here,
    field_ref,
    lhs,
    weights,
    corner_lhs,
    corner_weights,
    mats,
    send_sem,
    recv_sem,
    sum_send,
    sum_recv,
    load_sem,
):
    me = lax.axis_index("row")
    barrier = pltpu.get_barrier_semaphore()

    def greet(step, carry):
        pl.semaphore_signal(barrier, inc=1, device_id={"row": lax.rem(me + step, n)})
        return carry

    lax.fori_loop(1, n, greet, 0)

    loads = [
        pltpu.make_async_copy(source, target, load_sem.at[slot])
        for slot, (source, target) in enumerate(
            (
                (prior_ref.at[0], prior_here),
                (cols_ref.at[0, 0, 1], east_near),
                (cols_ref.at[0, 1, 0], east_far),
                (rows_ref.at[0], rows_here),
            )
        )
    ]
    for load in loads:
        load.start()

    has_below = jnp.where(me < n - 1, 1, 0)
    has_above = jnp.where(me > 0, 1, 0)

    def up(source, target, slot):
        return pltpu.make_async_remote_copy(
            src_ref=source,
            dst_ref=target,
            send_sem=send_sem.at[slot],
            recv_sem=recv_sem.at[slot],
            device_id={"row": lax.rem(me + n - 1, n)},
        )

    def down(source, target, slot):
        return pltpu.make_async_remote_copy(
            src_ref=source,
            dst_ref=target,
            send_sem=send_sem.at[slot],
            recv_sem=recv_sem.at[slot],
            device_id={"row": lax.rem(me + 1, n)},
        )

    def exchange(ups, downs, zeros_below, zeros_above):
        @pl.when(me > 0)
        def _():
            for copy in ups:
                copy.start()

        @pl.when(me < n - 1)
        def _():
            for copy in downs:
                copy.start()

        @pl.when(me == n - 1)
        def _():
            for ref in zeros_below:
                ref[...] = jnp.zeros_like(ref)

        @pl.when(me == 0)
        def _():
            for ref in zeros_above:
                ref[...] = jnp.zeros_like(ref)

    def arrive(ups, downs):
        @pl.when(me < n - 1)
        def _():
            for copy in ups:
                copy.wait_recv()

        @pl.when(me > 0)
        def _():
            for copy in downs:
                copy.wait_recv()

    def leave(ups, downs):
        @pl.when(me > 0)
        def _():
            for copy in ups:
                copy.wait_send()

        @pl.when(me < n - 1)
        def _():
            for copy in downs:
                copy.wait_send()

    select = edge_matrix()
    field_ref[...] = jnp.zeros_like(field_ref)
    pl.semaphore_wait(barrier, n - 1)
    ups_wide = (up(rows_ref.at[0, :, 0], below_ref, 0),)
    downs_wide = (down(rows_ref.at[0, :, 1], above_ref, 2),)
    exchange(ups_wide, downs_wide, (below_ref,), (above_ref,))

    loads[0].wait()
    for tile in range(2):
        for colour in range(3):
            for p in range(4):
                spot = p * 8 + tile * 4 + colour
                field_ref[spot : spot + 1, :] = prior_here[tile, colour, p : p + 1, :]
    row = iota((32, NODES), 0)
    unit = jnp.where(((row & 3) == (row >> 3)) & ((row & 3) < 3), 1.0, 0.0)
    rhs = 0.5 * (unit + field_ref[...])
    edges = joined(dot_nt(thirds(rhs), select))
    head_ref[:META, :] = edges
    for tile in range(2):
        for direction in range(4):
            spot = META + tile * 12 + direction * 3
            numbers = (
                off_ref[0, tile, direction],
                ext_ref[0, tile, 0, direction],
                ext_ref[0, tile, 1, direction],
            )
            for which, number in enumerate(numbers):
                head_ref[spot + which : spot + which + 1, :] = jnp.full(
                    (1, LANES), number, jnp.int32
                ).astype(F32)

    ups = (up(head_ref, below_head, 1),)
    downs = (down(head_ref, above_head, 3),)
    exchange(ups, downs, (below_head,), (above_head,))
    ups = ups + ups_wide
    downs = downs + downs_wide

    offset = meta_row(head_ref, 0, 0, 0, SIDE)
    low = meta_row(head_ref, 0, 0, 1, SIDE)
    high = meta_row(head_ref, 0, 0, 2, SIDE)
    loads[1].wait()
    loads[2].wait()
    east_a = flat(east_near[...])
    east_b = aligned(flat(east_far[...]), offset)
    put_products(lhs, 0, 0, east_a, east_b)
    put_products(lhs, 1, 0, east_b, east_a)
    put_weights(weights, 0, 0, 2 * G, False, offset, low, high, 1)
    put_weights(weights, 1, 0, 3 * G, True, offset, low, high, 1)
    for tile in range(2):
        offset = meta_row(head_ref, tile, 1, 0, SIDE)
        low = meta_row(head_ref, tile, 1, 1, SIDE)
        high = meta_row(head_ref, tile, 1, 2, SIDE)
        put_weights(weights, tile, SIDE, 0, False, offset, low, high, has_below)
    image = smooth(rhs)

    loads[3].wait()
    arrive(ups, downs)
    last = slice(SIDE - LANES, SIDE)
    first = slice(0, LANES)
    for tile in range(2):
        offset = meta_row(head_ref, tile, 1, 0, SIDE)
        south_a = flat(rows_here[tile, 1])
        south_b = aligned(flat(below_ref[tile]), offset)
        put_products(lhs, tile, SIDE, south_a, south_b)

        offset = meta_row(above_head, tile, 1, 0, SIDE)
        low = meta_row(above_head, tile, 1, 1, SIDE)
        high = meta_row(above_head, tile, 1, 2, SIDE)
        north_a = flat(above_ref[tile])
        north_b = aligned(flat(rows_here[tile, 0]), offset)
        put_products(lhs, tile, 2 * SIDE, north_b, north_a)
        put_weights(weights, tile, 2 * SIDE, G, True, offset, low, high, has_above)

        direction = 2 + tile
        offset = meta_row(head_ref, tile, direction, 0, LANES)
        low = meta_row(head_ref, tile, direction, 1, LANES)
        high = meta_row(head_ref, tile, direction, 2, LANES)
        if tile == 0:
            corner_a = roll(flat(rows_here[0, 1, :, :, last]), CELL, 1)
            corner_b = flat(below_ref[1, :, :, first])
        else:
            corner_a = flat(rows_here[1, 1, :, :, first])
            corner_b = roll(flat(below_ref[0, :, :, last]), CELL, 1)
        put_products(corner_lhs, tile, 0, corner_a, aligned(corner_b, offset))
        spot = G - 1 if tile == 0 else 0
        put_corner_weights(corner_weights, tile, 0, spot, offset, low, high, has_below)

        direction = 3 - tile
        offset = meta_row(above_head, 1 - tile, direction, 0, LANES)
        low = meta_row(above_head, 1 - tile, direction, 1, LANES)
        high = meta_row(above_head, 1 - tile, direction, 2, LANES)
        if tile == 0:
            corner_a = flat(above_ref[1, :, :, first])
            corner_b = roll(flat(rows_here[0, 0, :, :, last]), CELL, 1)
        else:
            corner_a = roll(flat(above_ref[0, :, :, last]), CELL, 1)
            corner_b = flat(rows_here[1, 0, :, :, first])
        put_products(corner_lhs, tile, LANES, aligned(corner_b, offset), corner_a)
        spot = 2 * G - 1 if tile == 0 else G
        put_corner_weights(corner_weights, tile, LANES, spot, offset, low, high, has_above)

    plain = [folded(dot_nt(lhs[tile], weights[tile])) for tile in range(2)]
    extra = [folded(dot_nt(corner_lhs[tile], corner_weights[tile])) for tile in range(2)]
    top = iota((KINDS, 8, LANES), 1) < 4
    none = jnp.where(top, plain[0][..., :LANES], plain[1][..., :LANES])
    one = jnp.where(top, plain[0][..., LANES:], plain[1][..., LANES:])
    corner = jnp.where(top, extra[0], extra[1])
    whole = none + one + corner
    for q in range(4):
        for kind, values, index in (
            (0, whole, xx_kind),
            (1, -none, xy_kind),
            (2, -one, xy_kind),
            (3, -corner, xy_kind),
        ):
            mats[kind, q] = jnp.concatenate([values[index(p, q)] for p in range(4)], axis=0)

    terms = pair_terms(mats, edges, below_head[:META, :], above_head[:META, :])
    image = image + joined(dot_nn(thirds(terms), select))
    edges = joined(dot_nt(thirds(image), select))
    edge_ref[...] = edges
    ups_edge = (up(edge_ref, below_edge, 4),)
    downs_edge = (down(edge_ref, above_edge, 5),)
    exchange(ups_edge, downs_edge, (below_edge,), (above_edge,))

    lane = iota((8, LANES), 1)
    row = iota((8, LANES), 0)
    spread = (lane == (row & 3)) & (lane < 3)

    def as_row(column):
        return jnp.sum(jnp.where(spread & (row < 4), column, 0.0), axis=0, keepdims=True)

    def as_column(values):
        column = jnp.sum(jnp.where(spread, values, 0.0), axis=1, keepdims=True)
        return jnp.concatenate([column] * 4, axis=0)

    rr = by_colour(rhs * rhs)
    rq = by_colour(rhs * image)
    theta = jnp.clip(jnp.where(rr > 0.0, rq / jnp.where(rr > 0.0, rr, 1.0), 0.0), 0.0, 20.0)
    tilt = per_row(theta)
    bent = image - tilt * rhs
    ru = by_colour(rhs * bent)
    uu = by_colour(bent * bent)

    second = smooth(image)
    arrive(ups_edge, downs_edge)
    terms = pair_terms(mats, edges, below_edge[...], above_edge[...])
    second = second + joined(dot_nn(thirds(terms), select))
    twice = second - tilt * image
    rv = by_colour(rhs * twice)
    uv = by_colour(bent * twice)
    parts = [as_row(value) for value in (rr, rq, ru, uu, rv, uv, theta)]
    sums_ref[me] = jnp.concatenate(parts + [jnp.zeros((1, LANES), F32)], axis=0)

    def sum_copy(step, owner):
        return pltpu.make_async_remote_copy(
            src_ref=sums_ref.at[me],
            dst_ref=sums_ref.at[owner],
            send_sem=sum_send.at[step],
            recv_sem=sum_recv.at[step],
            device_id={"row": lax.rem(me + step, n)},
        )

    def send(step, carry):
        sum_copy(step, me).start()
        return carry

    def receive(step, carry):
        sum_copy(step, lax.rem(me + n - step, n)).wait_recv()
        return carry

    lax.fori_loop(1, n, send, 0)
    lax.fori_loop(1, n, receive, 0)
    rr, rq, ru, uu, rv, uv, theta = [sums_ref[:, spot, :] for spot in range(7)]

    def total(values):
        return jnp.sum(values, axis=0, keepdims=True)

    real = iota((1, LANES), 1) < 3
    norm = jnp.where(real, total(rr), 1.0)
    curvature = jnp.where(real, total(rq), 1.0)
    alpha = norm / curvature
    keep = 1.0 - alpha * theta
    uq = uu + theta * ru
    norm_next = total(keep * keep * rr - 2.0 * alpha * keep * ru + alpha * alpha * uu)
    with_image = total(keep * rq - alpha * uq)
    with_lifted = total(keep * keep * rq - alpha * keep * (rv + uq) + alpha * alpha * uv)
    beta = norm_next / norm
    bend = with_lifted + 2.0 * beta * with_image + beta * beta * curvature
    alpha_next = norm_next / jnp.where(real, bend, 1.0)
    step = as_column(alpha)
    step_next = as_column(alpha_next)
    turn = as_column(beta)
    residual = rhs - step * image
    lifted = image - step * second
    answer = step * rhs + step_next * (residual + turn * rhs)
    left = residual - step_next * (lifted + turn * image)
    for tile in range(2):
        for colour in range(3):
            for p in range(4):
                spot = p * 8 + tile * 4 + colour
                x_ref[0, tile, colour, p : p + 1, :] = answer[spot : spot + 1]
                res_ref[0, tile, colour, p : p + 1, :] = left[spot : spot + 1]

    leave(ups, downs)
    leave(ups_edge, downs_edge)

    def sent(step, carry):
        sum_copy(step, me).wait_send()
        return carry

    lax.fori_loop(1, n, sent, 0)


def on_device(n, rows_strip, cols_strip, offsets, extents, prior):
    vmem = pl.BlockSpec(memory_space=pltpu.VMEM)
    hbm = pl.BlockSpec(memory_space=pltpu.HBM)
    smem = pl.BlockSpec(memory_space=pltpu.SMEM)
    shape = jax.ShapeDtypeStruct(prior.shape, F32)
    margins = rows_strip.shape[1:2] + rows_strip.shape[3:]
    return pl.pallas_call(
        functools.partial(kernel, n),
        out_shape=(shape, shape),
        in_specs=[hbm, hbm, smem, smem, hbm],
        out_specs=(vmem, vmem),
        scratch_shapes=[
            pltpu.VMEM(margins, BF16),
            pltpu.VMEM(margins, BF16),
            pltpu.VMEM((META + 24, LANES), F32),
            pltpu.VMEM((META + 24, LANES), F32),
            pltpu.VMEM((META + 24, LANES), F32),
            pltpu.VMEM((META, LANES), F32),
            pltpu.VMEM((META, LANES), F32),
            pltpu.VMEM((META, LANES), F32),
            pltpu.VMEM((n, 8, LANES), F32),
            pltpu.VMEM(rows_strip.shape[1:], BF16),
            pltpu.VMEM(cols_strip.shape[3:], BF16),
            pltpu.VMEM(cols_strip.shape[3:], BF16),
            pltpu.VMEM(prior.shape[1:], F32),
            pltpu.VMEM((32, NODES), F32),
            pltpu.VMEM((2, 2 * ROWS, 3 * SIDE), BF16),
            pltpu.VMEM((2, 2 * LANES, 3 * SIDE), BF16),
            pltpu.VMEM((2, 2 * ROWS, 2 * LANES), BF16),
            pltpu.VMEM((2, LANES, 2 * LANES), BF16),
            pltpu.VMEM((4, 4, 32, LANES), F32),
            pltpu.SemaphoreType.DMA((6,)),
            pltpu.SemaphoreType.DMA((6,)),
            pltpu.SemaphoreType.DMA((n,)),
            pltpu.SemaphoreType.DMA((n,)),
            pltpu.SemaphoreType.DMA((4,)),
        ],
        compiler_params=pltpu.CompilerParams(
            collective_id=0, has_side_effects=True, vmem_limit_bytes=64 * 1024 * 1024
        ),
    )(rows_strip, cols_strip, offsets, extents.swapaxes(2, 3), prior)


def solution(mesh):
    return jax.shard_map(
        functools.partial(on_device, mesh.shape["row"]),
        mesh=mesh,
        in_specs=(
            P(("slab", "row"), None, None, None, None, None),
            P(("slab", "row"), None, None, None, None, None),
            P(("slab", "row"), None, None),
            P(("slab", "row"), None, None, None),
            P(("slab", "row"), None, None, None, None),
        ),
        out_specs=(
            P(("slab", "row"), None, None, None, None),
            P(("slab", "row"), None, None, None, None),
        ),
        check_vma=False,
    )
```

```python
import functools

import jax
import jax.numpy as jnp
from jax import lax
from jax.experimental import pallas as pl
from jax.experimental.pallas import tpu as pltpu
from jax.sharding import PartitionSpec as P

G = 32
CELL = 16
NODES = G * G
SIDE = G * CELL
LANES = 128
KINDS = 22
ROWS = KINDS * 8
META = 32

F32 = jnp.float32
BF16 = jnp.bfloat16


def iota(shape, axis):
    return lax.broadcasted_iota(jnp.int32, shape, axis)


def roll(values, shift, axis):
    return pltpu.roll(values, shift % values.shape[axis], axis)


def dot_nt(first, second):
    return lax.dot_general(first, second, (((1,), (1,)), ((), ())), preferred_element_type=F32)


def dot_nn(first, second):
    return lax.dot_general(first, second, (((1,), (0,)), ((), ())), preferred_element_type=F32)


def thirds(values):
    high = values.astype(BF16)
    rest = values - high.astype(F32)
    middle = rest.astype(BF16)
    low = (rest - middle.astype(F32)).astype(BF16)
    return jnp.concatenate([high, middle, low], axis=0)


def joined(parts):
    size = parts.shape[0] // 3
    return parts[:size] + (parts[size : 2 * size] + parts[2 * size :])


def edge_matrix():
    lane = iota((LANES, NODES), 0)
    node = iota((LANES, NODES), 1)
    spot = lane & (G - 1)
    target = jnp.where(
        lane < G,
        NODES - G + spot,
        jnp.where(lane < 2 * G, spot, jnp.where(lane < 3 * G, spot * G + G - 1, spot * G)),
    )
    return jnp.where(node == target, 1.0, 0.0).astype(BF16)


def smooth(field):
    node = iota((1, NODES), 1)
    column = node & (G - 1)
    up = jnp.where(node >= G, 1.0, 0.0)
    down = jnp.where(node < NODES - G, 1.0, 0.0)
    left = jnp.where(column > 0, 1.0, 0.0)
    right = jnp.where(column < G - 1, 1.0, 0.0)
    total = (0.5 + up + down + left + right) * field
    total = total - up * roll(field, G, 1) - down * roll(field, -G, 1)
    return total - left * roll(field, 1, 1) - right * roll(field, -1, 1)


def meta_row(buffer, tile, direction, which, width):
    spot = META + tile * 12 + direction * 3 + which
    row = buffer[spot : spot + 1, :].astype(jnp.int32)
    return jnp.concatenate([row] * (width // LANES), axis=1)


def aligned(strip, offset):
    amount = jnp.broadcast_to(offset, strip.shape)
    for bit in range(4):
        strip = jnp.where((amount & (1 << bit)) != 0, roll(strip, -(1 << bit), 1), strip)
    return strip


def flat(strip):
    return strip.astype(F32).reshape(3 * CELL, strip.shape[-1])


def put_products(lhs, tile, start, x, y):
    width = x.shape[-1]
    x = x.reshape(3, CELL, width)
    y = y.reshape(3, CELL, width)
    products = jnp.concatenate(
        [
            x[0:1] * x,
            x[1:2] * x[1:],
            x[2:3] * x[2:],
            x,
            x[0:1] * y,
            x[1:2] * y,
            x[2:3] * y,
            y,
            jnp.ones((1, CELL, width), F32),
        ],
        axis=0,
    )
    sums = (products[:, :8] + products[:, 8:]).reshape(ROWS, width)
    high = sums.astype(BF16)
    lhs[tile, :ROWS, start : start + width] = high
    lhs[tile, ROWS:, start : start + width] = (sums - high.astype(F32)).astype(BF16)


def put_weights(weights, tile, start, base, at_b, offset, low, high, exists):
    place = iota((1, SIDE), 1)
    moved = place + offset
    valid = (place >= low) & (place < high) & (moved < SIDE)
    split = (moved >> 4) - (place >> 4)
    cell = (moved >> 4) if at_b else (place >> 4)
    target = jnp.where(valid, base + cell + LANES * split, -1)
    target = jnp.where(exists > 0, target, -1)
    hit = iota((2 * LANES, SIDE), 0) == jnp.broadcast_to(target, (2 * LANES, SIDE))
    weights[tile, :, start : start + SIDE] = jnp.where(hit, 1.0 / (CELL * CELL), 0.0).astype(BF16)


def put_corner_weights(weights, tile, start, lane, offset, low, high, exists):
    place = iota((1, LANES), 1)
    valid = (place >= low) & (place < high) & (place + offset < CELL)
    target = jnp.where(valid, lane, -1)
    target = jnp.where(exists > 0, target, -1)
    hit = iota((LANES, LANES), 0) == jnp.broadcast_to(target, (LANES, LANES))
    weights[tile, :, start : start + LANES] = jnp.where(hit, 1.0 / (CELL * CELL), 0.0).astype(BF16)


def folded(parts):
    parts = (parts[:ROWS] + parts[ROWS:]).reshape(KINDS, 8, parts.shape[-1])
    return jnp.broadcast_to(jnp.sum(parts, axis=1, keepdims=True), parts.shape)


def xx_kind(p, q):
    p, q = min(p, q), max(p, q)
    if p == 3:
        return 21
    if q == 3:
        return 6 + p
    return (0, 3, 5)[p] + q - p


def xy_kind(p, q):
    if p == 3 and q == 3:
        return 21
    if q == 3:
        return 6 + p
    if p == 3:
        return 18 + q
    return 9 + 3 * p + q


def pair_terms(mats, edges, below, above):
    lane = iota((8, LANES), 1)
    row = iota((8, LANES), 0)
    at_a = (lane & G) == 0
    total = jnp.zeros((32, LANES), F32)
    for q in range(4):
        rows = slice(8 * q, 8 * q + 8)
        own = edges[rows]
        other = roll(own, 4, 0)
        near = jnp.where(
            lane < G,
            roll(below[rows], -G, 1),
            jnp.where(
                lane < 2 * G,
                roll(above[rows], G, 1),
                jnp.where(lane < 3 * G, roll(other, -G, 1), roll(other, G, 1)),
            ),
        )
        moved = jnp.where(at_a, roll(near, -1, 1), roll(near, 1, 1))
        swapped = roll(near, 4, 0)
        corner = jnp.where(row < 4, roll(swapped, G - 1, 1), roll(swapped, 1 - G, 1))
        for kind, values in enumerate((own, near, moved, corner)):
            total = total + mats[kind, q] * jnp.concatenate([values] * 4, axis=0)
    return total


def by_colour(values):
    narrow = values[:, :LANES]
    for start in range(LANES, NODES, LANES):
        narrow = narrow + values[:, start : start + LANES]
    narrow = (narrow[0:8] + narrow[8:16]) + (narrow[16:24] + narrow[24:32])
    return jnp.sum(narrow + roll(narrow, 4, 0), axis=1, keepdims=True)


def per_row(values):
    return jnp.concatenate([values] * 4, axis=0)


def kernel(
    n,
    rows_ref,
    cols_ref,
    off_ref,
    ext_ref,
    prior_ref,
    x_ref,
    res_ref,
    below_ref,
    above_ref,
    head_ref,
    below_head,
    above_head,
    edge_ref,
    below_edge,
    above_edge,
    sums_ref,
    rows_here,
    east_near,
    east_far,
    prior_here,
    field_ref,
    lhs,
    weights,
    corner_lhs,
    corner_weights,
    mats,
    send_sem,
    recv_sem,
    sum_send,
    sum_recv,
    load_sem,
):
    me = lax.axis_index("row")
    barrier = pltpu.get_barrier_semaphore()

    def greet(step, carry):
        pl.semaphore_signal(barrier, inc=1, device_id={"row": lax.rem(me + step, n)})
        return carry

    lax.fori_loop(1, n, greet, 0)

    loads = [
        pltpu.make_async_copy(source, target, load_sem.at[slot])
        for slot, (source, target) in enumerate(
            (
                (prior_ref.at[0], prior_here),
                (cols_ref.at[0, 0, 1], east_near),
                (cols_ref.at[0, 1, 0], east_far),
                (rows_ref.at[0], rows_here),
            )
        )
    ]
    for load in loads:
        load.start()

    has_below = jnp.where(me < n - 1, 1, 0)
    has_above = jnp.where(me > 0, 1, 0)

    def up(source, target, slot):
        return pltpu.make_async_remote_copy(
            src_ref=source,
            dst_ref=target,
            send_sem=send_sem.at[slot],
            recv_sem=recv_sem.at[slot],
            device_id={"row": lax.rem(me + n - 1, n)},
        )

    def down(source, target, slot):
        return pltpu.make_async_remote_copy(
            src_ref=source,
            dst_ref=target,
            send_sem=send_sem.at[slot],
            recv_sem=recv_sem.at[slot],
            device_id={"row": lax.rem(me + 1, n)},
        )

    def exchange(ups, downs, zeros_below, zeros_above):
        @pl.when(me > 0)
        def _():
            for copy in ups:
                copy.start()

        @pl.when(me < n - 1)
        def _():
            for copy in downs:
                copy.start()

        @pl.when(me == n - 1)
        def _():
            for ref in zeros_below:
                ref[...] = jnp.zeros_like(ref)

        @pl.when(me == 0)
        def _():
            for ref in zeros_above:
                ref[...] = jnp.zeros_like(ref)

    def arrive(ups, downs):
        @pl.when(me < n - 1)
        def _():
            for copy in ups:
                copy.wait_recv()

        @pl.when(me > 0)
        def _():
            for copy in downs:
                copy.wait_recv()

    def leave(ups, downs):
        @pl.when(me > 0)
        def _():
            for copy in ups:
                copy.wait_send()

        @pl.when(me < n - 1)
        def _():
            for copy in downs:
                copy.wait_send()

    select = edge_matrix()
    field_ref[...] = jnp.zeros_like(field_ref)
    pl.semaphore_wait(barrier, n - 1)
    ups_wide = (up(rows_ref.at[0, :, 0], below_ref, 0),)
    downs_wide = (down(rows_ref.at[0, :, 1], above_ref, 2),)
    exchange(ups_wide, downs_wide, (below_ref,), (above_ref,))

    loads[0].wait()
    for tile in range(2):
        for colour in range(3):
            for p in range(4):
                spot = p * 8 + tile * 4 + colour
                field_ref[spot : spot + 1, :] = prior_here[tile, colour, p : p + 1, :]
    row = iota((32, NODES), 0)
    unit = jnp.where(((row & 3) == (row >> 3)) & ((row & 3) < 3), 1.0, 0.0)
    rhs = 0.5 * (unit + field_ref[...])
    edges = joined(dot_nt(thirds(rhs), select))
    head_ref[:META, :] = edges
    for tile in range(2):
        for direction in range(4):
            spot = META + tile * 12 + direction * 3
            numbers = (
                off_ref[0, tile, direction],
                ext_ref[0, tile, 0, direction],
                ext_ref[0, tile, 1, direction],
            )
            for which, number in enumerate(numbers):
                head_ref[spot + which : spot + which + 1, :] = jnp.full(
                    (1, LANES), number, jnp.int32
                ).astype(F32)

    ups = (up(head_ref, below_head, 1),)
    downs = (down(head_ref, above_head, 3),)
    exchange(ups, downs, (below_head,), (above_head,))
    ups = ups + ups_wide
    downs = downs + downs_wide

    offset = meta_row(head_ref, 0, 0, 0, SIDE)
    low = meta_row(head_ref, 0, 0, 1, SIDE)
    high = meta_row(head_ref, 0, 0, 2, SIDE)
    loads[1].wait()
    loads[2].wait()
    east_a = flat(east_near[...])
    east_b = aligned(flat(east_far[...]), offset)
    put_products(lhs, 0, 0, east_a, east_b)
    put_products(lhs, 1, 0, east_b, east_a)
    put_weights(weights, 0, 0, 2 * G, False, offset, low, high, 1)
    put_weights(weights, 1, 0, 3 * G, True, offset, low, high, 1)
    for tile in range(2):
        offset = meta_row(head_ref, tile, 1, 0, SIDE)
        low = meta_row(head_ref, tile, 1, 1, SIDE)
        high = meta_row(head_ref, tile, 1, 2, SIDE)
        put_weights(weights, tile, SIDE, 0, False, offset, low, high, has_below)
    image = smooth(rhs)
    smooth_edges = joined(dot_nt(thirds(image), select))

    loads[3].wait()
    arrive(ups, downs)
    last = slice(SIDE - LANES, SIDE)
    first = slice(0, LANES)
    for tile in range(2):
        offset = meta_row(head_ref, tile, 1, 0, SIDE)
        south_a = flat(rows_here[tile, 1])
        south_b = aligned(flat(below_ref[tile]), offset)
        put_products(lhs, tile, SIDE, south_a, south_b)

        offset = meta_row(above_head, tile, 1, 0, SIDE)
        low = meta_row(above_head, tile, 1, 1, SIDE)
        high = meta_row(above_head, tile, 1, 2, SIDE)
        north_a = flat(above_ref[tile])
        north_b = aligned(flat(rows_here[tile, 0]), offset)
        put_products(lhs, tile, 2 * SIDE, north_b, north_a)
        put_weights(weights, tile, 2 * SIDE, G, True, offset, low, high, has_above)

        direction = 2 + tile
        offset = meta_row(head_ref, tile, direction, 0, LANES)
        low = meta_row(head_ref, tile, direction, 1, LANES)
        high = meta_row(head_ref, tile, direction, 2, LANES)
        if tile == 0:
            corner_a = roll(flat(rows_here[0, 1, :, :, last]), CELL, 1)
            corner_b = flat(below_ref[1, :, :, first])
        else:
            corner_a = flat(rows_here[1, 1, :, :, first])
            corner_b = roll(flat(below_ref[0, :, :, last]), CELL, 1)
        put_products(corner_lhs, tile, 0, corner_a, aligned(corner_b, offset))
        spot = G - 1 if tile == 0 else 0
        put_corner_weights(corner_weights, tile, 0, spot, offset, low, high, has_below)

        direction = 3 - tile
        offset = meta_row(above_head, 1 - tile, direction, 0, LANES)
        low = meta_row(above_head, 1 - tile, direction, 1, LANES)
        high = meta_row(above_head, 1 - tile, direction, 2, LANES)
        if tile == 0:
            corner_a = flat(above_ref[1, :, :, first])
            corner_b = roll(flat(rows_here[0, 0, :, :, last]), CELL, 1)
        else:
            corner_a = roll(flat(above_ref[0, :, :, last]), CELL, 1)
            corner_b = flat(rows_here[1, 0, :, :, first])
        put_products(corner_lhs, tile, LANES, aligned(corner_b, offset), corner_a)
        spot = 2 * G - 1 if tile == 0 else G
        put_corner_weights(corner_weights, tile, LANES, spot, offset, low, high, has_above)

    plain = [folded(dot_nt(lhs[tile], weights[tile])) for tile in range(2)]
    extra = [folded(dot_nt(corner_lhs[tile], corner_weights[tile])) for tile in range(2)]
    top = iota((KINDS, 8, LANES), 1) < 4
    none = jnp.where(top, plain[0][..., :LANES], plain[1][..., :LANES])
    one = jnp.where(top, plain[0][..., LANES:], plain[1][..., LANES:])
    corner = jnp.where(top, extra[0], extra[1])
    whole = none + one + corner
    for q in range(4):
        for kind, values, index in (
            (0, whole, xx_kind),
            (1, -none, xy_kind),
            (2, -one, xy_kind),
            (3, -corner, xy_kind),
        ):
            mats[kind, q] = jnp.concatenate([values[index(p, q)] for p in range(4)], axis=0)

    terms = pair_terms(mats, edges, below_head[:META, :], above_head[:META, :])
    shared = dot_nt(select, select).astype(BF16)
    edges = smooth_edges + joined(dot_nn(thirds(terms), shared))
    edge_ref[...] = edges
    ups_edge = (up(edge_ref, below_edge, 4),)
    downs_edge = (down(edge_ref, above_edge, 5),)
    exchange(ups_edge, downs_edge, (below_edge,), (above_edge,))
    image = image + joined(dot_nn(thirds(terms), select))

    lane = iota((8, LANES), 1)
    row = iota((8, LANES), 0)
    spread = (lane == (row & 3)) & (lane < 3)

    def as_row(column):
        return jnp.sum(jnp.where(spread & (row < 4), column, 0.0), axis=0, keepdims=True)

    def as_column(values):
        column = jnp.sum(jnp.where(spread, values, 0.0), axis=1, keepdims=True)
        return jnp.concatenate([column] * 4, axis=0)

    rr = by_colour(rhs * rhs)
    rq = by_colour(rhs * image)
    theta = jnp.clip(jnp.where(rr > 0.0, rq / jnp.where(rr > 0.0, rr, 1.0), 0.0), 0.0, 20.0)
    tilt = per_row(theta)
    bent = image - tilt * rhs
    ru = by_colour(rhs * bent)
    uu = by_colour(bent * bent)

    second = smooth(image)
    arrive(ups_edge, downs_edge)
    terms = pair_terms(mats, edges, below_edge[...], above_edge[...])
    second = second + joined(dot_nn(thirds(terms), select))
    twice = second - tilt * image
    rv = by_colour(rhs * twice)
    uv = by_colour(bent * twice)
    parts = [as_row(value) for value in (rr, rq, ru, uu, rv, uv, theta)]
    sums_ref[me] = jnp.concatenate(parts + [jnp.zeros((1, LANES), F32)], axis=0)

    def sum_copy(step, owner):
        return pltpu.make_async_remote_copy(
            src_ref=sums_ref.at[me],
            dst_ref=sums_ref.at[owner],
            send_sem=sum_send.at[step],
            recv_sem=sum_recv.at[step],
            device_id={"row": lax.rem(me + step, n)},
        )

    def send(step, carry):
        sum_copy(step, me).start()
        return carry

    def receive(step, carry):
        sum_copy(step, lax.rem(me + n - step, n)).wait_recv()
        return carry

    lax.fori_loop(1, n, send, 0)
    lax.fori_loop(1, n, receive, 0)
    rr, rq, ru, uu, rv, uv, theta = [sums_ref[:, spot, :] for spot in range(7)]

    def total(values):
        return jnp.sum(values, axis=0, keepdims=True)

    real = iota((1, LANES), 1) < 3
    norm = jnp.where(real, total(rr), 1.0)
    curvature = jnp.where(real, total(rq), 1.0)
    alpha = norm / curvature
    keep = 1.0 - alpha * theta
    uq = uu + theta * ru
    norm_next = total(keep * keep * rr - 2.0 * alpha * keep * ru + alpha * alpha * uu)
    with_image = total(keep * rq - alpha * uq)
    with_lifted = total(keep * keep * rq - alpha * keep * (rv + uq) + alpha * alpha * uv)
    beta = norm_next / norm
    bend = with_lifted + 2.0 * beta * with_image + beta * beta * curvature
    alpha_next = norm_next / jnp.where(real, bend, 1.0)
    step = as_column(alpha)
    step_next = as_column(alpha_next)
    turn = as_column(beta)
    residual = rhs - step * image
    lifted = image - step * second
    answer = step * rhs + step_next * (residual + turn * rhs)
    left = residual - step_next * (lifted + turn * image)
    for tile in range(2):
        for colour in range(3):
            for p in range(4):
                spot = p * 8 + tile * 4 + colour
                x_ref[0, tile, colour, p : p + 1, :] = answer[spot : spot + 1]
                res_ref[0, tile, colour, p : p + 1, :] = left[spot : spot + 1]

    leave(ups, downs)
    leave(ups_edge, downs_edge)

    def sent(step, carry):
        sum_copy(step, me).wait_send()
        return carry

    lax.fori_loop(1, n, sent, 0)


def on_device(n, rows_strip, cols_strip, offsets, extents, prior):
    vmem = pl.BlockSpec(memory_space=pltpu.VMEM)
    hbm = pl.BlockSpec(memory_space=pltpu.HBM)
    smem = pl.BlockSpec(memory_space=pltpu.SMEM)
    shape = jax.ShapeDtypeStruct(prior.shape, F32)
    margins = rows_strip.shape[1:2] + rows_strip.shape[3:]
    return pl.pallas_call(
        functools.partial(kernel, n),
        out_shape=(shape, shape),
        in_specs=[hbm, hbm, smem, smem, hbm],
        out_specs=(vmem, vmem),
        scratch_shapes=[
            pltpu.VMEM(margins, BF16),
            pltpu.VMEM(margins, BF16),
            pltpu.VMEM((META + 24, LANES), F32),
            pltpu.VMEM((META + 24, LANES), F32),
            pltpu.VMEM((META + 24, LANES), F32),
            pltpu.VMEM((META, LANES), F32),
            pltpu.VMEM((META, LANES), F32),
            pltpu.VMEM((META, LANES), F32),
            pltpu.VMEM((n, 8, LANES), F32),
            pltpu.VMEM(rows_strip.shape[1:], BF16),
            pltpu.VMEM(cols_strip.shape[3:], BF16),
            pltpu.VMEM(cols_strip.shape[3:], BF16),
            pltpu.VMEM(prior.shape[1:], F32),
            pltpu.VMEM((32, NODES), F32),
            pltpu.VMEM((2, 2 * ROWS, 3 * SIDE), BF16),
            pltpu.VMEM((2, 2 * LANES, 3 * SIDE), BF16),
            pltpu.VMEM((2, 2 * ROWS, 2 * LANES), BF16),
            pltpu.VMEM((2, LANES, 2 * LANES), BF16),
            pltpu.VMEM((4, 4, 32, LANES), F32),
            pltpu.SemaphoreType.DMA((6,)),
            pltpu.SemaphoreType.DMA((6,)),
            pltpu.SemaphoreType.DMA((n,)),
            pltpu.SemaphoreType.DMA((n,)),
            pltpu.SemaphoreType.DMA((4,)),
        ],
        compiler_params=pltpu.CompilerParams(
            collective_id=0, has_side_effects=True, vmem_limit_bytes=64 * 1024 * 1024
        ),
    )(rows_strip, cols_strip, offsets, extents.swapaxes(2, 3), prior)


def solution(mesh):
    return jax.shard_map(
        functools.partial(on_device, mesh.shape["row"]),
        mesh=mesh,
        in_specs=(
            P(("slab", "row"), None, None, None, None, None),
            P(("slab", "row"), None, None, None, None, None),
            P(("slab", "row"), None, None),
            P(("slab", "row"), None, None, None),
            P(("slab", "row"), None, None, None, None),
        ),
        out_specs=(
            P(("slab", "row"), None, None, None, None),
            P(("slab", "row"), None, None, None, None),
        ),
        check_vma=False,
    )
```
